32 devices in a mesh: batch: 8 (over y, x, core), proto: 4 (over z).
Axes of the slice: x: 2, y: 2, z: 4, core: 2. Of those that a mesh axis runs over, the one named last changes fastest.
Arguments:
- features: bfloat16 [2, 8192, 256], P(None, 'batch'), may hold values from -6 to 6
- prototypes: bfloat16 [32768, 256], P('proto'), may hold values from -6 to 6
Outputs:
- grad_features: float32 [2, 8192, 256], P(None, 'batch')
- grad_prototypes: float32 [32768, 256], P('proto')
The draws below stay inside these ranges and needn't reach their ends.
All inputs are finite; a program needn't handle non-finite values.
Results may differ from the reference program's by a relative error of at most 0.0027.
Values sent between devices are 32-bit elements; how exact they have to be, the bound alone decides.
No kernel may reach another device: no remote copies, remote signals or barrier semaphores. Data moves between devices by JAX's collectives and lax.ppermute only.
A program may use at most 384 MiB of HBM per device.

```python
import math
import jax
import jax.numpy as jnp
from jax import lax

D = 256
K = 32768
ITERS = 3
B = 8192


def shared_direction(key):
    picks = jax.random.randint(jax.random.fold_in(key, 101), (D,), 0, 2)
    return jnp.where(picks > 0, 1.0, -1.0).astype(jnp.float32)


def draw_features(key, part):
    direction = shared_direction(key)
    key_sign = jax.random.fold_in(key, 11)
    key_rough = jax.random.fold_in(key, 12)
    key_amount = jax.random.fold_in(key, 13)
    picks = jax.random.randint(key_sign, (1, B, 1), 0, 5)
    polarity = jnp.where(picks < 4, 1.0, -1.0).astype(jnp.float32)
    rough = jax.random.normal(key_rough, (2, B, D), jnp.float32)
    amount = jax.random.uniform(key_amount, (2, B, 1), jnp.float32, 0.25, 0.47)
    values = rough + amount * polarity * direction[None, None, :]
    return jnp.clip(values, -6.0, 6.0).astype(jnp.bfloat16)


def draw_prototypes(key, part):
    direction = shared_direction(key)
    key_sign = jax.random.fold_in(key, 21)
    key_rough = jax.random.fold_in(key, 22)
    key_amount = jax.random.fold_in(key, 23)
    picks = jax.random.randint(key_sign, (K, 1), 0, 5)
    polarity = jnp.where(picks < 2, 1.0, -1.0).astype(jnp.float32)
    rough = jax.random.normal(key_rough, (K, D), jnp.float32)
    amount = jax.random.uniform(key_amount, (K, 1), jnp.float32, 0.25, 0.47)
    values = rough + amount * polarity * direction[None, :]
    return jnp.clip(values, -6.0, 6.0).astype(jnp.bfloat16)


def setup_inputs(seed: int = 0) -> dict:
    key_list = jax.random.split(jax.random.key(seed), 3)
    features = draw_features(jax.random.fold_in(key_list[2], 71), 0)
    prototypes = draw_prototypes(jax.random.fold_in(key_list[2], 71), 0)
    return {"features": features, "prototypes": prototypes}


code_temp = 0.05
soft_temp = 0.1

def norm_back(grad, unit, inverse):
    return inverse * (grad - unit * lax.optimization_barrier(jnp.sum(unit * grad, axis=-1, keepdims=True)))

def reference(features, prototypes):
    rows_view = features.shape[1]
    width = features.shape[2]
    feat = features.astype(jnp.float32)
    inv_feat = lax.rsqrt(lax.optimization_barrier(jnp.sum(feat * feat, axis=-1, keepdims=True)) + 1e-06)
    unit_feat = feat * inv_feat
    embed = unit_feat.astype(jnp.bfloat16)
    proto = prototypes.astype(jnp.float32)
    inv_proto = lax.rsqrt(lax.optimization_barrier(jnp.sum(proto * proto, axis=-1, keepdims=True)) + 1e-06)
    unit_proto = proto * inv_proto
    centers = unit_proto.astype(jnp.bfloat16)
    centers_t = centers.T
    block = math.gcd(rows_view, 512)
    nblocks = rows_view // block
    blocks = embed.reshape(2, nblocks, block, width)

    def scores_of(rows):
        return jnp.dot(rows, centers_t, preferred_element_type=jnp.float32)
    row_scale = jnp.ones((2, nblocks, block), jnp.float32)
    col_list = [None, None]
    for step in range(ITERS):
        new_cols = []
        new_rows = []
        for view in range(2):

            def col_step(carry, item):
                rows, weights = item
                base = jnp.exp(scores_of(rows) / code_temp)
                return (carry + lax.optimization_barrier(jnp.sum(base * weights[:, None], axis=0)), None)
            total, unused = lax.scan(col_step, jnp.zeros((centers.shape[0],), jnp.float32), (blocks[view], row_scale[view]))
            col_scale = 1.0 / total

            def row_step(carry, rows):
                base = jnp.exp(scores_of(rows) / code_temp)
                return (carry, 1.0 / lax.optimization_barrier(jnp.sum(base * col_scale[None, :], axis=1)))
            unused, rscale = lax.scan(row_step, 0.0, blocks[view])
            new_cols.append(col_scale)
            new_rows.append(rscale)
        col_list = new_cols
        row_scale = jnp.stack(new_rows)
    col_scale = jnp.stack(col_list)

    def grad_step(carry, item):
        rows_pair, rscale = item
        grads = []
        codes = []
        probs = []
        for view in range(2):
            scores = scores_of(rows_pair[view])
            base = jnp.exp(scores / code_temp)
            codes.append(base * rscale[view][:, None] * col_scale[view][None, :])
            expo = jnp.exp(scores / soft_temp)
            probs.append(expo / lax.optimization_barrier(jnp.sum(expo, axis=1, keepdims=True)))
        outs = []
        for view in range(2):
            grad_scores = ((probs[view] - codes[1 - view]) * (0.5 / soft_temp)).astype(jnp.bfloat16)
            outs.append(jnp.dot(grad_scores, centers, preferred_element_type=jnp.float32))
            carry = carry + jnp.dot(grad_scores.T, rows_pair[view], preferred_element_type=jnp.float32)
        return (carry, jnp.stack(outs))
    pairs = jnp.transpose(blocks, (1, 0, 2, 3))
    rpairs = jnp.transpose(row_scale, (1, 0, 2))
    grad_centers, grad_embed = lax.scan(grad_step, jnp.zeros((centers.shape[0], width), jnp.float32), (pairs, rpairs))
    grad_embed = jnp.transpose(grad_embed, (1, 0, 2, 3)).reshape(2, rows_view, width)
    grad_features = norm_back(grad_embed, unit_feat, inv_feat)
    grad_prototypes = norm_back(grad_centers, unit_proto, inv_proto)
    return (grad_features, grad_prototypes)
```

```python
import jax
import jax.numpy as jnp
from jax import lax
from jax.experimental import pallas as pl
from jax.experimental.pallas import tpu as pltpu
from jax.sharding import PartitionSpec as P

ITERS = 3
LOG2E = 1.4426950408889634
SOFT = 10.0 * LOG2E
GRAD = 5.0
F32 = jnp.float32
BF16 = jnp.bfloat16
NT = (((1,), (1,)), ((), ()))


def tile_of(n, most):
    t = most
    while n % t:
        t //= 2
    return t


def params(mib):
    return pltpu.CompilerParams(vmem_limit_bytes=mib * 2**20)


def lane_fold(x):
    total = x[:, :128]
    for j in range(1, x.shape[1] // 128):
        total = total + x[:, 128 * j : 128 * (j + 1)]
    return total


def sub_fold(x):
    total = x[:8]
    for j in range(1, x.shape[0] // 8):
        total = total + x[8 * j : 8 * (j + 1)]
    return total


def spread(row):
    return jnp.broadcast_to(row, (128, row.shape[1])).T


def unit_of(x):
    inv = lax.rsqrt(jnp.sum(x * x, axis=-1, keepdims=True) + 1e-06)
    return x * inv, inv


def first_kernel(feat_ref, proto_ref, embed_ref, cent_ref, base_ref, col_ref, tot_ref, soft_ref, acc):
    i = pl.program_id(0)
    rows = feat_ref.shape[1]
    kt = proto_ref.shape[0]
    rc = tile_of(rows, 256)

    @pl.when(i == 0)
    def _():
        acc[...] = jnp.zeros_like(acc)
        soft_ref[...] = jnp.zeros_like(soft_ref)
        for v in range(2):
            embed_ref[v] = unit_of(feat_ref[v].astype(F32))[0].astype(BF16)

    cent_ref[...] = unit_of(proto_ref[...].astype(F32))[0].astype(BF16)
    for v in range(2):

        def step(j, col):
            r = pl.ds(pl.multiple_of(j * rc, rc), rc)
            s = lax.dot_general(embed_ref[v, r, :], cent_ref[...], NT, preferred_element_type=F32)
            e = jnp.exp2(s * SOFT)
            acc[v, r, :] += lane_fold(e)
            soft_ref[v, r, :] += jnp.dot(e.astype(BF16), cent_ref[...], preferred_element_type=F32)
            b = e * e
            base_ref[v, r, :] = b.astype(BF16)
            return col + sub_fold(b)

        col = lax.fori_loop(0, rows // rc, step, jnp.zeros((8, kt), F32), unroll=True)
        col_ref[v, pl.ds(i, 1), :] = jnp.sum(col, axis=0, keepdims=True)

    @pl.when(i == pl.num_programs(0) - 1)
    def _():
        for v in range(2):
            tot_ref[v : v + 1, :] = jnp.sum(acc[v].T, axis=0, keepdims=True)


def first(features, prototypes):
    _, rows, width = features.shape
    protos = prototypes.shape[0]
    kt = tile_of(protos, 1024)
    n = protos // kt
    whole = lambda *s: pl.BlockSpec(s, lambda i: (0,) * len(s))
    return pl.pallas_call(
        first_kernel,
        grid=(n,),
        in_specs=[whole(2, rows, width), pl.BlockSpec((kt, width), lambda i: (i, 0))],
        out_specs=[
            whole(2, rows, width),
            pl.BlockSpec((kt, width), lambda i: (i, 0)),
            pl.BlockSpec((2, rows, kt), lambda i: (0, 0, i)),
            whole(2, n, kt),
            whole(2, rows),
            whole(2, rows, width),
        ],
        out_shape=[
            jax.ShapeDtypeStruct((2, rows, width), BF16),
            jax.ShapeDtypeStruct((protos, width), BF16),
            jax.ShapeDtypeStruct((2, rows, protos), BF16),
            jax.ShapeDtypeStruct((2, n, kt), F32),
            jax.ShapeDtypeStruct((2, rows), F32),
            jax.ShapeDtypeStruct((2, rows, width), F32),
        ],
        scratch_shapes=[pltpu.VMEM((2, rows, 128), F32)],
        compiler_params=params(48),
        name="first",
    )(features, prototypes)


def row_kernel(base_ref, *refs):
    *part_refs, out_ref, acc = refs
    i = pl.program_id(0)
    rows = base_ref.shape[1]
    rc = 16

    @pl.when(i == 0)
    def _():
        acc[...] = jnp.zeros_like(acc)

    for v in range(2):
        c = 1.0 / sum(p[v, pl.ds(i, 1), :] for p in part_refs)

        def step(j, carry):
            r = pl.ds(pl.multiple_of(j * rc, rc), rc)
            acc[v, r, :] += lane_fold(base_ref[v, r, :].astype(F32) * c)
            return carry

        lax.fori_loop(0, rows // rc, step, 0, unroll=4)

    @pl.when(i == pl.num_programs(0) - 1)
    def _():
        for v in range(2):
            out_ref[v : v + 1, :] = jnp.sum(acc[v].T, axis=0, keepdims=True)


def row_last_kernel(base_ref, cent_ref, *refs):
    *part_refs, out_ref, code_ref, acc = refs
    i = pl.program_id(0)
    rows = base_ref.shape[1]
    rc = tile_of(rows, 256)

    @pl.when(i == 0)
    def _():
        acc[...] = jnp.zeros_like(acc)
        code_ref[...] = jnp.zeros_like(code_ref)

    for v in range(2):
        c = 1.0 / sum(p[v, pl.ds(i, 1), :] for p in part_refs)

        def step(j, carry):
            r = pl.ds(pl.multiple_of(j * rc, rc), rc)
            w = base_ref[v, r, :].astype(F32) * c
            acc[v, r, :] += lane_fold(w)
            code_ref[v, r, :] += jnp.dot(w.astype(BF16), cent_ref[...], preferred_element_type=F32)
            return carry

        lax.fori_loop(0, rows // rc, step, 0, unroll=True)

    @pl.when(i == pl.num_programs(0) - 1)
    def _():
        for v in range(2):
            out_ref[v : v + 1, :] = jnp.sum(acc[v].T, axis=0, keepdims=True)


def row_pass(base, parts, centers=None):
    _, rows, protos = base.shape
    _, n, kt = parts[0].shape
    whole = lambda *s: pl.BlockSpec(s, lambda i: (0,) * len(s))
    in_specs = [pl.BlockSpec((2, rows, kt), lambda i: (0, 0, i))]
    out_specs = [whole(2, rows)]
    out_shape = [jax.ShapeDtypeStruct((2, rows), F32)]
    args = [base]
    if centers is not None:
        width = centers.shape[1]
        in_specs.append(pl.BlockSpec((kt, width), lambda i: (i, 0)))
        out_specs.append(whole(2, rows, width))
        out_shape.append(jax.ShapeDtypeStruct((2, rows, width), F32))
        args.append(centers)
    return pl.pallas_call(
        row_kernel if centers is None else row_last_kernel,
        grid=(n,),
        in_specs=in_specs + [whole(2, n, kt)] * len(parts),
        out_specs=out_specs,
        out_shape=out_shape,
        scratch_shapes=[pltpu.VMEM((2, rows, 128), F32)],
        compiler_params=params(48),
        name="row_pass" if centers is None else "row_last",
    )(*args, *parts)


def col_kernel(base_ref, total_ref, out_ref, scale):
    i = pl.program_id(0)
    rows, kt = base_ref.shape[1:]
    rc = 16

    @pl.when(i == 0)
    def _():
        for v in range(2):
            scale[v] = spread(1.0 / total_ref[v : v + 1, :])

    for v in range(2):

        def step(j, col):
            r = pl.ds(pl.multiple_of(j * rc, rc), rc)
            w = jnp.concatenate([scale[v, r, :]] * (kt // 128), axis=1)
            return col + sub_fold(base_ref[v, r, :].astype(F32) * w)

        col = lax.fori_loop(0, rows // rc, step, jnp.zeros((8, kt), F32), unroll=4)
        out_ref[v, pl.ds(i, 1), :] = jnp.sum(col, axis=0, keepdims=True)


def col_pass(base, total, n):
    _, rows, protos = base.shape
    kt = protos // n
    whole = lambda *s: pl.BlockSpec(s, lambda i: (0,) * len(s))
    return pl.pallas_call(
        col_kernel,
        grid=(n,),
        in_specs=[pl.BlockSpec((2, rows, kt), lambda i: (0, 0, i)), whole(2, rows)],
        out_specs=whole(2, n, kt),
        out_shape=jax.ShapeDtypeStruct((2, n, kt), F32),
        scratch_shapes=[pltpu.VMEM((2, rows, 128), F32)],
        compiler_params=params(48),
        name="col_pass",
    )(base, total)


def grad_kernel(cent_ref, embed_ref, tot_ref, row_ref, col_ref, out_ref, scale):
    rows = embed_ref.shape[1]
    kt = cent_ref.shape[0]
    rc = tile_of(rows, 512)
    for v in range(2):
        scale[v] = spread(col_ref[v, pl.ds(pl.program_id(0), 1), :])
    cs = [jnp.concatenate([scale[v]] * (rc // 128), axis=1) for v in range(2)]
    total = jnp.zeros(out_ref.shape, F32)
    for j in range(rows // rc):
        r = slice(j * rc, (j + 1) * rc)
        es = []
        for v in range(2):
            s = lax.dot_general(cent_ref[...], embed_ref[v, r, :], NT, preferred_element_type=F32)
            es.append(jnp.exp2(s * SOFT))
        for v in range(2):
            o = 1 - v
            codes = es[o] * es[o] * (GRAD / row_ref[o : o + 1, r]) * cs[o]
            g = (es[v] * (GRAD / tot_ref[v : v + 1, r]) - codes).astype(BF16)
            total = total + jnp.dot(g, embed_ref[v, r, :], preferred_element_type=F32)
    out_ref[...] = total


def grad_pass(centers, embed, tot, row, col):
    protos, width = centers.shape
    rows = embed.shape[1]
    kt = tile_of(protos, 512)
    n = protos // kt
    whole = lambda *s: pl.BlockSpec(s, lambda i: (0,) * len(s))
    return pl.pallas_call(
        grad_kernel,
        grid=(n,),
        in_specs=[
            pl.BlockSpec((kt, width), lambda i: (i, 0)),
            whole(2, rows, width),
            whole(2, rows),
            whole(2, rows),
            whole(2, n, kt),
        ],
        out_specs=pl.BlockSpec((kt, width), lambda i: (i, 0)),
        out_shape=jax.ShapeDtypeStruct((protos, width), F32),
        scratch_shapes=[pltpu.VMEM((2, kt, 128), F32)],
        compiler_params=params(48),
        name="grad_pass",
    )(centers, embed, tot, row, col.reshape(2, n, kt))


def swap(x, axis, n, m):
    return lax.ppermute(x, axis, [(i, i ^ m) for i in range(n)])


def col_exchange(x, n):
    if n > 1:
        x = x + swap(x, "batch", n, 1)
    m = 2
    while n // m > 4:
        x = x + swap(x, "batch", n, m)
        m *= 2
    return [x] + [swap(x, "batch", n, k * m) for k in range(1, n // m)]


def row_exchange(x, n):
    m = 1
    while m < n:
        x = x + swap(x, "proto", n, m)
        m *= 2
    return x


def norm_back(grad, unit, inverse):
    return inverse * (grad - unit * jnp.sum(unit * grad, axis=-1, keepdims=True))


def per_device(nb, npr, features, prototypes):
    embed, centers, base, col, tot, soft = first(features, prototypes)
    n = col.shape[1]
    parts = col_exchange(col, nb)
    tot = row_exchange(tot, npr)
    for step in range(ITERS - 1):
        (row,) = row_pass(base, parts)
        row = row_exchange(row, npr)
        parts = col_exchange(col_pass(base, row, n), nb)
    row, code = row_pass(base, parts, centers)
    row = row_exchange(row, npr)
    col = 1.0 / sum(parts)
    grad_embed = soft * (GRAD / tot)[:, :, None] - (code * (GRAD / row)[:, :, None])[::-1]
    grad_embed = lax.psum(grad_embed, "proto")
    grad_centers = lax.psum(grad_pass(centers, embed, tot, row, col), "batch")
    unit_feat, inv_feat = unit_of(features.astype(F32))
    unit_proto, inv_proto = unit_of(prototypes.astype(F32))
    return (
        norm_back(grad_embed, unit_feat, inv_feat),
        norm_back(grad_centers, unit_proto, inv_proto),
    )


def solution(mesh):
    nb, npr = mesh.shape["batch"], mesh.shape["proto"]
    return jax.shard_map(
        lambda f, p: per_device(nb, npr, f, p),
        mesh=mesh,
        in_specs=(P(None, "batch", None), P("proto", None)),
        out_specs=(P(None, "batch", None), P("proto", None)),
        check_vma=False,
    )
```

```python
import jax
import jax.numpy as jnp
from jax import lax
from jax.experimental import pallas as pl
from jax.experimental.pallas import tpu as pltpu
from jax.sharding import PartitionSpec as P

ITERS = 3
LOG2E = 1.4426950408889634
SOFT = 10.0 * LOG2E
GRAD = 5.0
F32 = jnp.float32
BF16 = jnp.bfloat16
NT = (((1,), (1,)), ((), ()))


def tile_of(n, most):
    t = most
    while n % t:
        t //= 2
    return t


def params(mib):
    return pltpu.CompilerParams(vmem_limit_bytes=mib * 2**20)


def cost(flops, nbytes):
    return pl.CostEstimate(flops=flops, bytes_accessed=nbytes, transcendentals=0)


def lane_fold(x):
    total = x[:, :128]
    for j in range(1, x.shape[1] // 128):
        total = total + x[:, 128 * j : 128 * (j + 1)]
    return total


def sub_fold(x):
    total = x[:8]
    for j in range(1, x.shape[0] // 8):
        total = total + x[8 * j : 8 * (j + 1)]
    return total


def spread(row):
    return jnp.broadcast_to(row, (128, row.shape[1])).T


def unit_of(x):
    inv = lax.rsqrt(jnp.sum(x * x, axis=-1, keepdims=True) + 1e-06)
    return x * inv, inv


def first_kernel(
    feat_ref, proto_ref, lo_ref, hi_ref, cent_ref, base_ref, col_ref, tot_ref, soft_ref, acc, embed_ref
):
    i = pl.program_id(0)
    rows = feat_ref.shape[1]
    kt = proto_ref.shape[0]
    rc = tile_of(rows, 256)

    @pl.when(i == 0)
    def _():
        acc[...] = jnp.zeros_like(acc)
        soft_ref[...] = jnp.zeros_like(soft_ref)
        for v in range(2):
            e = unit_of(feat_ref[v].astype(F32))[0].astype(BF16)
            embed_ref[v] = e
            lo_ref[v] = e[: rows // 2].astype(F32)
            hi_ref[v] = e[rows // 2 :].astype(F32)

    cent_ref[...] = unit_of(proto_ref[...].astype(F32))[0].astype(BF16)
    for v in range(2):

        def step(j, col):
            r = pl.ds(pl.multiple_of(j * rc, rc), rc)
            s = lax.dot_general(embed_ref[v, r, :], cent_ref[...], NT, preferred_element_type=F32)
            e = jnp.exp2(s * SOFT)
            acc[v, r, :] += lane_fold(e)
            soft_ref[v, r, :] += jnp.dot(e.astype(BF16), cent_ref[...], preferred_element_type=F32)
            b = e * e
            base_ref[0, v, r, :] = b.astype(BF16)
            return col + sub_fold(b)

        col = lax.fori_loop(0, rows // rc, step, jnp.zeros((8, kt), F32), unroll=True)
        col_ref[v, pl.ds(i, 1), :] = jnp.sum(col, axis=0, keepdims=True)

    @pl.when(i == pl.num_programs(0) - 1)
    def _():
        for v in range(2):
            tot_ref[v : v + 1, :] = jnp.sum(acc[v].T, axis=0, keepdims=True)


def first(features, prototypes):
    _, rows, width = features.shape
    protos = prototypes.shape[0]
    kt = tile_of(protos, 1024)
    n = protos // kt
    whole = lambda *s: pl.BlockSpec(s, lambda i: (0,) * len(s))
    return pl.pallas_call(
        first_kernel,
        grid=(n,),
        in_specs=[whole(2, rows, width), pl.BlockSpec((kt, width), lambda i: (i, 0))],
        out_specs=[
            whole(2, rows // 2, width),
            whole(2, rows // 2, width),
            pl.BlockSpec((kt, width), lambda i: (i, 0)),
            pl.BlockSpec((1, 2, rows, kt), lambda i: (i, 0, 0, 0)),
            whole(2, n, kt),
            whole(2, rows),
            whole(2, rows, width),
        ],
        out_shape=[
            jax.ShapeDtypeStruct((2, rows // 2, width), F32),
            jax.ShapeDtypeStruct((2, rows // 2, width), F32),
            jax.ShapeDtypeStruct((protos, width), BF16),
            jax.ShapeDtypeStruct((n, 2, rows, kt), BF16),
            jax.ShapeDtypeStruct((2, n, kt), F32),
            jax.ShapeDtypeStruct((2, rows), F32),
            jax.ShapeDtypeStruct((2, rows, width), F32),
        ],
        scratch_shapes=[pltpu.VMEM((2, rows, 128), F32), pltpu.VMEM((2, rows, width), BF16)],
        compiler_params=params(48),
        cost_estimate=cost(16 * rows * protos * width, 4 * rows * protos),
        name="first",
    )(features, prototypes)


def row_kernel(base_ref, *refs):
    *part_refs, out_ref, acc = refs
    i = pl.program_id(0)
    rows = base_ref.shape[2]
    rc = 16

    @pl.when(i == 0)
    def _():
        acc[...] = jnp.zeros_like(acc)

    for v in range(2):
        c = 1.0 / sum(p[v, pl.ds(i, 1), :] for p in part_refs)

        def step(j, carry):
            r = pl.ds(pl.multiple_of(j * rc, rc), rc)
            acc[v, r, :] += lane_fold(base_ref[0, v, r, :].astype(F32) * c)
            return carry

        lax.fori_loop(0, rows // rc, step, 0, unroll=4)

    @pl.when(i == pl.num_programs(0) - 1)
    def _():
        for v in range(2):
            out_ref[v : v + 1, :] = jnp.sum(acc[v].T, axis=0, keepdims=True)


def row_last_kernel(base_ref, cent_ref, *refs):
    *part_refs, out_ref, code_ref, acc = refs
    i = pl.program_id(0)
    rows = base_ref.shape[2]
    rc = tile_of(rows, 256)

    @pl.when(i == 0)
    def _():
        acc[...] = jnp.zeros_like(acc)
        code_ref[...] = jnp.zeros_like(code_ref)

    for v in range(2):
        c = 1.0 / sum(p[v, pl.ds(i, 1), :] for p in part_refs)

        def step(j, carry):
            r = pl.ds(pl.multiple_of(j * rc, rc), rc)
            w = base_ref[0, v, r, :].astype(F32) * c
            acc[v, r, :] += lane_fold(w)
            code_ref[v, r, :] += jnp.dot(w.astype(BF16), cent_ref[...], preferred_element_type=F32)
            return carry

        lax.fori_loop(0, rows // rc, step, 0, unroll=True)

    @pl.when(i == pl.num_programs(0) - 1)
    def _():
        for v in range(2):
            out_ref[v : v + 1, :] = jnp.sum(acc[v].T, axis=0, keepdims=True)


def row_pass(base, parts, centers=None):
    n, _, rows, kt = base.shape
    whole = lambda *s: pl.BlockSpec(s, lambda i: (0,) * len(s))
    in_specs = [pl.BlockSpec((1, 2, rows, kt), lambda i: (i, 0, 0, 0))]
    out_specs = [whole(2, rows)]
    out_shape = [jax.ShapeDtypeStruct((2, rows), F32)]
    args = [base]
    if centers is not None:
        width = centers.shape[1]
        in_specs.append(pl.BlockSpec((kt, width), lambda i: (i, 0)))
        out_specs.append(whole(2, rows, width))
        out_shape.append(jax.ShapeDtypeStruct((2, rows, width), F32))
        args.append(centers)
    return pl.pallas_call(
        row_kernel if centers is None else row_last_kernel,
        grid=(n,),
        in_specs=in_specs + [whole(2, n, kt)] * len(parts),
        out_specs=out_specs,
        out_shape=out_shape,
        scratch_shapes=[pltpu.VMEM((2, rows, 128), F32)],
        compiler_params=params(48),
        cost_estimate=cost(0, 8 * n * rows * kt),
        name="row_pass" if centers is None else "row_last",
    )(*args, *parts)


def col_kernel(base_ref, total_ref, out_ref, scale):
    i = pl.program_id(0)
    rows, kt = base_ref.shape[2:]
    rc = 16

    @pl.when(i == 0)
    def _():
        for v in range(2):
            scale[v] = spread(1.0 / total_ref[v : v + 1, :])

    for v in range(2):

        def step(j, col):
            r = pl.ds(pl.multiple_of(j * rc, rc), rc)
            w = jnp.concatenate([scale[v, r, :]] * (kt // 128), axis=1)
            return col + sub_fold(base_ref[0, v, r, :].astype(F32) * w)

        col = lax.fori_loop(0, rows // rc, step, jnp.zeros((8, kt), F32), unroll=4)
        out_ref[v, pl.ds(i, 1), :] = jnp.sum(col, axis=0, keepdims=True)


def col_pass(base, total):
    n, _, rows, kt = base.shape
    whole = lambda *s: pl.BlockSpec(s, lambda i: (0,) * len(s))
    return pl.pallas_call(
        col_kernel,
        grid=(n,),
        in_specs=[pl.BlockSpec((1, 2, rows, kt), lambda i: (i, 0, 0, 0)), whole(2, rows)],
        out_specs=whole(2, n, kt),
        out_shape=jax.ShapeDtypeStruct((2, n, kt), F32),
        scratch_shapes=[pltpu.VMEM((2, rows, 128), F32)],
        compiler_params=params(48),
        cost_estimate=cost(0, 8 * n * rows * kt),
        name="col_pass",
    )(base, total)


def pack_kernel(*refs):
    *part_refs, out_ref = refs
    for j, p in enumerate(part_refs):
        out_ref[j] = p[...].astype(BF16)


def pack(parts):
    _, rc, width = parts[0].shape
    m = len(parts)
    return pl.pallas_call(
        pack_kernel,
        grid=(2,),
        in_specs=[pl.BlockSpec((1, rc, width), lambda v: (v, 0, 0))] * m,
        out_specs=pl.BlockSpec((m, 1, rc, width), lambda v: (0, v, 0, 0)),
        out_shape=jax.ShapeDtypeStruct((m, 2, rc, width), BF16),
        compiler_params=params(32),
        cost_estimate=cost(0, 12 * m * rc * width),
        name="pack",
    )(*parts)


def grad_kernel(cent_ref, col_ref, embed, *refs):
    *row_refs, out_ref, scale = refs
    m, _, rc, _ = embed.shape
    i = pl.program_id(0)
    for v in range(2):
        scale[v] = spread(col_ref[v, pl.ds(i, 1), :])
    total = jnp.zeros(out_ref.shape, F32)
    for j in range(m):
        es = []
        for v in range(2):
            s = lax.dot_general(cent_ref[...], embed[j, v], NT, preferred_element_type=F32)
            es.append(jnp.exp2(s * SOFT))
        for v in range(2):
            o = 1 - v
            c = jnp.concatenate([scale[o]] * (rc // 128), axis=1)
            r = slice(j % 2 * rc, (j % 2 + 1) * rc)
            codes = es[o] * es[o] * (GRAD / row_refs[m // 2 + j // 2][o : o + 1, r]) * c
            g = (es[v] * (GRAD / row_refs[j // 2][v : v + 1, r]) - codes).astype(BF16)
            total = total + jnp.dot(g, embed[j, v], preferred_element_type=F32)
    out_ref[...] = total


def grad_pass(centers, embeds, tot, row, col):
    protos, width = centers.shape
    m, _, rc, _ = embeds.shape
    kt = tile_of(protos, 512)
    n = protos // kt
    whole = lambda *s: pl.BlockSpec(s, lambda i: (0,) * len(s))
    return pl.pallas_call(
        grad_kernel,
        grid=(n,),
        in_specs=[
            pl.BlockSpec((kt, width), lambda i: (i, 0)),
            whole(2, n, kt),
            whole(m, 2, rc, width),
        ]
        + [whole(2, 2 * rc)] * m,
        out_specs=pl.BlockSpec((kt, width), lambda i: (i, 0)),
        out_shape=jax.ShapeDtypeStruct((protos, width), F32),
        scratch_shapes=[pltpu.VMEM((2, kt, 128), F32)],
        compiler_params=params(48),
        cost_estimate=cost(8 * protos * m * rc * width, 4 * m * rc * width),
        name="grad_pass",
    )(centers, col.reshape(2, n, kt), embeds, *tot, *row)


def place_kernel(at_ref, *refs):
    m = len(refs) - 2
    out_ref, sems = refs[m], refs[m + 1]
    copies = []
    for j in range(m):
        size = refs[j].shape[0]
        where = pl.ds(pl.multiple_of(at_ref[j], 8), size)
        copies.append(pltpu.make_async_copy(refs[j], out_ref.at[where], sems.at[j]))
    for c in copies:
        c.start()
    for c in copies:
        c.wait()


def place(pieces, at, size):
    m = len(pieces)
    return pl.pallas_call(
        place_kernel,
        in_specs=[pl.BlockSpec(memory_space=pltpu.SMEM)]
        + [pl.BlockSpec(memory_space=pltpu.VMEM)] * m,
        out_specs=pl.BlockSpec(memory_space=pl.ANY),
        out_shape=jax.ShapeDtypeStruct((size, pieces[0].shape[1]), F32),
        scratch_shapes=[pltpu.SemaphoreType.DMA((m,))],
        compiler_params=params(24),
        name="place",
    )(jnp.stack(at).astype(jnp.int32), *pieces)


def swap(x, axis, n, m):
    return lax.ppermute(x, axis, [(i, i ^ m) for i in range(n)])


def col_exchange(x, n):
    if n > 1:
        x = x + swap(x, "batch", n, 1)
    m = 2
    while n // m > 4:
        x = x + swap(x, "batch", n, m)
        m *= 2
    return [x] + [swap(x, "batch", n, k * m) for k in range(1, n // m)]


def row_exchange(x, n):
    m = 1
    while m < n:
        x = x + swap(x, "proto", n, m)
        m *= 2
    return x


def gather_plan(n):
    bits = [2**j for j in range(1, n.bit_length()) if 2**j < n]
    plan, keys_a, keys_b = [], [0], [0]
    for m, w in zip(bits, bits[::-1]):
        plan += [((k, m), (q, w)) for k, q in zip(keys_a, keys_b)]
        keys_a, keys_b = keys_a + [k ^ m for k in keys_a], keys_b + [k ^ w for k in keys_b]
    return plan


def send_pair(have, pair, n):
    for h, (k, m) in zip(have, pair):
        h[k ^ m] = swap(h[k], "batch", n, m)


def gather_rows(x, n):
    return [x] + [swap(x, "batch", n, k) for k in range(2, n, 2)]


def norm_back(grad, given):
    x = given.astype(F32)
    inverse = lax.rsqrt(jnp.sum(x * x, axis=-1, keepdims=True) + 1e-06)
    unit = x * inverse
    return inverse * (grad - unit * jnp.sum(unit * grad, axis=-1, keepdims=True))


def cut(x, at, size):
    return lax.dynamic_slice_in_dim(x, at, size, axis=0)


def halve_over_proto(x, n, m=1):
    size = x.shape[0] // 2
    side = (lax.axis_index("proto") // m) % 2
    return cut(x, side * size, size), swap(cut(x, (1 - side) * size, size), "proto", n, m)


def home(i, n, size):
    at = 0 * i
    for m in bits_of(n):
        size //= 2
        at = at + (i // m) % 2 * size
    return at


def spread_out(pieces, n):
    bits = bits_of(n)[::-1]
    keys = [0, bits[0]]
    size = pieces[0].shape[0]
    x = jnp.concatenate(pieces, axis=0)
    for m in bits[1:-1]:
        x = jnp.concatenate([x, swap(x, "proto", n, m)], axis=0)
        keys = keys + [k ^ m for k in keys]
    y = swap(x, "proto", n, bits[-1])
    found = {}
    for j, k in enumerate(keys):
        found[k] = x[j * size : (j + 1) * size]
        found[k ^ bits[-1]] = y[j * size : (j + 1) * size]
    return found


def bits_of(n):
    return [2**j for j in range(n.bit_length()) if 2**j < n]


def shard_back(pair, given, n):
    x = pair[0] + pair[1]
    for m in bits_of(n)[2:]:
        a, b = halve_over_proto(x, n, m)
        x = a + b
    at = home(lax.axis_index("proto"), n, given.shape[0])
    return norm_back(x, cut(given, at, x.shape[0]))


def per_device(nb, npr, features, prototypes):
    _, rows, width = features.shape
    protos = prototypes.shape[0]
    me = lax.axis_index("batch")
    chip, core = me // 2, me % 2
    share = protos // (nb // 2)

    lo, hi, centers, base, col, tot, soft = first(features, prototypes)
    parts = col_exchange(col, nb)
    tot = row_exchange(tot, npr)
    tots = gather_rows(tot, nb)
    have, plan = [{0: lo}, {0: hi}], gather_plan(nb)
    have, parts = lax.optimization_barrier((have, parts))
    for step in range(ITERS - 1):
        if plan:
            send_pair(have, plan.pop(0), nb)
        (row,) = row_pass(base, parts)
        col = col_pass(base, row_exchange(row, npr))
        col, have = lax.optimization_barrier((col, have))
        parts = col_exchange(col, nb)
        have, parts = lax.optimization_barrier((have, parts))
    for pair in plan:
        send_pair(have, pair, nb)
    row, code = row_pass(base, parts, centers)
    row = row_exchange(row, npr)
    row, have = lax.optimization_barrier((row, have))
    rows_all = gather_rows(row, nb)
    embeds = pack([have[h][k] for k in range(0, nb, 2) for h in range(2)])
    col = (1.0 / sum(parts)).reshape(2, protos)
    half = share // 2
    quarter = half // 2

    def grads(at):
        c = lax.dynamic_slice_in_dim(col, at, half, axis=1)
        return grad_pass(cut(centers, at, half), embeds, tots, rows_all, c)

    gf = [
        soft[v] * (GRAD / tot[v])[:, None] - code[1 - v] * (GRAD / row[1 - v])[:, None]
        for v in range(2)
    ]
    pair = halve_over_proto(gf[0], npr, 1)
    theirs = grads(chip * share + (1 - core) * half)
    theirs, pair, late = lax.optimization_barrier((theirs, pair, gf[1]))
    theirs = swap(theirs, "batch", nb, 1)
    pair = halve_over_proto(pair[0] + pair[1], npr, 2)
    pair_late = halve_over_proto(late, npr, 1)
    mine = grads(chip * share + core * half)
    mine, theirs, pair, pair_late = lax.optimization_barrier((mine, theirs, pair, pair_late))
    grad = norm_back(mine + theirs, cut(prototypes, chip * share + core * half, half))

    have, plan = [{0: grad[:quarter]}, {0: grad[quarter:]}], gather_plan(nb)
    last = bits_of(npr)[-1]
    send_pair(have, plan.pop(0), nb)
    shard = shard_back(pair, features[0], npr)
    near = swap(shard, "proto", npr, last)
    late = halve_over_proto(pair_late[0] + pair_late[1], npr, 2)
    have, near, late = lax.optimization_barrier((have, near, late))
    send_pair(have, plan.pop(0), nb)
    shards = [spread_out([shard, near], npr), shard_back(late, features[1], npr)]
    near = swap(shards[1], "proto", npr, last)
    have, near, first_view = lax.optimization_barrier((have, near, shards[0]))
    for p in plan:
        send_pair(have, p, nb)
    shards = [first_view, spread_out([shards[1], near], npr)]
    idx = lax.axis_index("proto")
    out, where = [], []
    for v in range(2):
        for k, x in shards[v].items():
            out.append(x)
            where.append(home(idx ^ k, npr, rows) + v * rows)
    grad_features = place(out, where, 2 * rows).reshape(2, rows, width)

    out, where = [], []
    for k in have[0]:
        for h in range(2):
            at = (chip ^ (k // 2)) * share + h * quarter
            out += [have[h][k], swap(have[h][k], "batch", nb, 1)]
            where += [at + core * half, at + (1 - core) * half]
    return grad_features, place(out, where, protos)


def solution(mesh):
    nb, npr = mesh.shape["batch"], mesh.shape["proto"]
    return jax.shard_map(
        lambda f, p: per_device(nb, npr, f, p),
        mesh=mesh,
        in_specs=(P(None, "batch", None), P("proto", None)),
        out_specs=(P(None, "batch", None), P("proto", None)),
        check_vma=False,
    )
```

```python
import jax
import jax.numpy as jnp
from jax import lax
from jax.experimental import pallas as pl
from jax.experimental.pallas import tpu as pltpu
from jax.sharding import PartitionSpec as P

ITERS = 3
LOG2E = 1.4426950408889634
SOFT = 10.0 * LOG2E
GRAD = 5.0
F32 = jnp.float32
BF16 = jnp.bfloat16
NT = (((1,), (1,)), ((), ()))


def tile_of(n, most):
    t = most
    while n % t:
        t //= 2
    return t


def params(mib):
    return pltpu.CompilerParams(vmem_limit_bytes=mib * 2**20)


def cost(flops, nbytes):
    return pl.CostEstimate(flops=flops, bytes_accessed=nbytes, transcendentals=0)


def lane_fold(x):
    total = x[:, :128]
    for j in range(1, x.shape[1] // 128):
        total = total + x[:, 128 * j : 128 * (j + 1)]
    return total


def sub_fold(x):
    total = x[:8]
    for j in range(1, x.shape[0] // 8):
        total = total + x[8 * j : 8 * (j + 1)]
    return total


def spread(row):
    return jnp.broadcast_to(row, (128, row.shape[1])).T


def unit_of(x):
    inv = lax.rsqrt(jnp.sum(x * x, axis=-1, keepdims=True) + 1e-06)
    return x * inv, inv


def two_terms(x):
    high = x.astype(BF16)
    return high, (x - high.astype(F32)).astype(BF16)


def in_vmem():
    return pl.BlockSpec(memory_space=pltpu.VMEM)


def first_kernel(feat_ref, proto_ref, lo_ref, hi_ref, cent_ref, col_ref, tot_ref, soft_ref, *refs):
    *base_refs, acc, embed_ref = refs
    i = pl.program_id(0)
    rows = feat_ref.shape[1]
    kt = proto_ref.shape[0]
    rc = base_refs[0].shape[1]

    @pl.when(i == 0)
    def _():
        acc[...] = jnp.zeros_like(acc)
        soft_ref[...] = jnp.zeros_like(soft_ref)
        for v in range(2):
            e = unit_of(feat_ref[v].astype(F32))[0].astype(BF16)
            embed_ref[v] = e
            lo_ref[v] = e[: rows // 2].astype(F32)
            hi_ref[v] = e[rows // 2 :].astype(F32)

    cent_ref[...] = unit_of(proto_ref[...].astype(F32))[0].astype(BF16)
    for v in range(2):
        col = jnp.zeros((8, kt), F32)
        for j in range(rows // rc):
            r = slice(j * rc, (j + 1) * rc)
            s = lax.dot_general(embed_ref[v, r, :], cent_ref[...], NT, preferred_element_type=F32)
            e = jnp.exp2(s * SOFT)
            acc[v, r, :] += lane_fold(e)
            soft_ref[v, r, :] += jnp.dot(e.astype(BF16), cent_ref[...], preferred_element_type=F32)
            b = e * e
            base_refs[v * (rows // rc) + j][i] = b.astype(BF16)
            col = col + sub_fold(b)
        col_ref[v, pl.ds(i, 1), :] = jnp.sum(col, axis=0, keepdims=True)

    @pl.when(i == pl.num_programs(0) - 1)
    def _():
        for v in range(2):
            tot_ref[v : v + 1, :] = jnp.sum(acc[v].T, axis=0, keepdims=True)


def first(features, prototypes):
    _, rows, width = features.shape
    protos = prototypes.shape[0]
    kt = tile_of(protos, 1024)
    n = protos // kt
    rc = tile_of(rows, 256)
    m = 2 * rows // rc
    outs = pl.pallas_call(
        first_kernel,
        grid=(n,),
        in_specs=[in_vmem(), pl.BlockSpec((kt, width), lambda i: (i, 0))],
        out_specs=[
            in_vmem(),
            in_vmem(),
            pl.BlockSpec((kt, width), lambda i: (i, 0)),
            in_vmem(),
            in_vmem(),
            in_vmem(),
        ]
        + [in_vmem()] * m,
        out_shape=[
            jax.ShapeDtypeStruct((2, rows // 2, width), F32),
            jax.ShapeDtypeStruct((2, rows // 2, width), F32),
            jax.ShapeDtypeStruct((protos, width), BF16),
            jax.ShapeDtypeStruct((2, n, kt), F32),
            jax.ShapeDtypeStruct((2, rows), F32),
            jax.ShapeDtypeStruct((2, rows, width), F32),
        ]
        + [pltpu.VMEM((n, rc, kt), BF16)] * m,
        scratch_shapes=[pltpu.VMEM((2, rows, 128), F32), pltpu.VMEM((2, rows, width), BF16)],
        compiler_params=params(16),
        cost_estimate=cost(16 * rows * protos * width, 0),
        name="first",
    )(features, prototypes)
    return outs[:6], outs[6:]


def load_scales(part_refs, rows_ref, cols_ref, v):
    n, kt = rows_ref.shape
    half = kt // 2
    for i in range(n):
        c = 1.0 / sum(p[v, i : i + 1, :] for p in part_refs)
        rows_ref[i : i + 1, :] = c
        high, low = two_terms(c[:, half:])
        cols_ref[i] = jnp.concatenate([high, low, jnp.zeros((126, half), BF16)], axis=0).T


def block_sum(base_ref, rows_ref, cols_ref, acc):
    n, rc, kt = base_ref.shape
    half = kt // 2
    total = jnp.dot(base_ref[0, :, half:], cols_ref[0], preferred_element_type=F32)
    for i in range(1, n):
        total = total + jnp.dot(base_ref[i, :, half:], cols_ref[i], preferred_element_type=F32)
    acc[...] = total
    step = 32
    for j in range(0, rc, step):
        r = slice(j, j + step)
        part = acc[r]
        for i in range(n):
            part = part + lane_fold(base_ref[i, r, :half].astype(F32) * rows_ref[i : i + 1, :half])
        acc[r] = part
    return jnp.sum(acc[...].T, axis=0, keepdims=True)


def row_kernel(m, *refs):
    base_refs, part_refs = refs[:m], refs[m:-4]
    out_ref, rows_ref, cols_ref, acc = refs[-4:]
    rc = base_refs[0].shape[1]
    for v in range(2):
        load_scales(part_refs, rows_ref, cols_ref, v)
        for j in range(m // 2):
            sums = block_sum(base_refs[v * (m // 2) + j], rows_ref, cols_ref, acc)
            out_ref[v : v + 1, j * rc : (j + 1) * rc] = sums


def row_last_kernel(m, *refs):
    base_refs, cent_ref, part_refs = refs[:m], refs[m], refs[m + 1 : -6]
    out_ref, code_ref, rows_ref, cols_ref, acc, scaled = refs[-6:]
    n, rc, kt = base_refs[0].shape
    for v in range(2):
        load_scales(part_refs, rows_ref, cols_ref, v)
        for i in range(n):
            c = spread(rows_ref[i : i + 1, :])
            c = jnp.concatenate([c] * (scaled.shape[2] // 128), axis=1)
            scaled[i] = (cent_ref[i * kt : (i + 1) * kt, :].astype(F32) * c).astype(BF16)
        for j in range(m // 2):
            base_ref = base_refs[v * (m // 2) + j]
            r = slice(j * rc, (j + 1) * rc)
            out_ref[v : v + 1, r] = block_sum(base_ref, rows_ref, cols_ref, acc)
            total = jnp.dot(base_ref[0], scaled[0], preferred_element_type=F32)
            for i in range(1, n):
                total = total + jnp.dot(base_ref[i], scaled[i], preferred_element_type=F32)
            code_ref[v, r, :] = total


def row_pass(base, parts, centers=None):
    m = len(base)
    n, rc, kt = base[0].shape
    rows = m // 2 * rc
    out_shape = [jax.ShapeDtypeStruct((2, rows), F32)]
    args = list(base)
    scratch = [
        pltpu.VMEM((n, kt), F32),
        pltpu.VMEM((n, kt // 2, 128), BF16),
        pltpu.VMEM((rc, 128), F32),
    ]
    kernel = row_kernel
    if centers is not None:
        width = centers.shape[1]
        out_shape.append(jax.ShapeDtypeStruct((2, rows, width), F32))
        args.append(centers)
        scratch.append(pltpu.VMEM((n, kt, width), BF16))
        kernel = row_last_kernel
    return pl.pallas_call(
        lambda *refs: kernel(m, *refs),
        in_specs=[in_vmem()] * (len(args) + len(parts)),
        out_specs=[in_vmem()] * len(out_shape),
        out_shape=out_shape,
        scratch_shapes=scratch,
        compiler_params=params(16),
        cost_estimate=cost(0, 4 * n * rows * kt),
        name="row_pass" if centers is None else "row_last",
    )(*args, *parts)


def col_kernel(total_ref, *refs):
    *base_refs, out_ref = refs
    m = len(base_refs) // 2
    n, rc, kt = base_refs[0].shape
    for v in range(2):
        high, low = two_terms(1.0 / total_ref[v : v + 1, :])
        r = jnp.concatenate([high, low, jnp.zeros((14, m * rc), BF16)], axis=0)
        for i in range(n):
            total = jnp.zeros((16, kt), F32)
            for j in range(m):
                total = total + jnp.dot(
                    r[:, j * rc : (j + 1) * rc],
                    base_refs[v * m + j][i],
                    preferred_element_type=F32,
                )
            out_ref[v, i : i + 1, :] = total[0:1] + total[1:2]


def col_pass(base, total):
    n, rc, kt = base[0].shape
    m = len(base)
    return pl.pallas_call(
        col_kernel,
        in_specs=[in_vmem()] * (m + 1),
        out_specs=in_vmem(),
        out_shape=jax.ShapeDtypeStruct((2, n, kt), F32),
        compiler_params=params(16),
        cost_estimate=cost(0, 4 * n * m // 2 * rc * kt),
        name="col_pass",
    )(total, *base)


def pack_kernel(*refs):
    *part_refs, out_ref = refs
    for j, p in enumerate(part_refs):
        out_ref[j] = p[...].astype(BF16)


def pack(parts):
    _, rc, width = parts[0].shape
    m = len(parts)
    return pl.pallas_call(
        pack_kernel,
        grid=(2,),
        in_specs=[pl.BlockSpec((1, rc, width), lambda v: (v, 0, 0))] * m,
        out_specs=pl.BlockSpec((m, 1, rc, width), lambda v: (0, v, 0, 0)),
        out_shape=jax.ShapeDtypeStruct((m, 2, rc, width), BF16),
        compiler_params=params(32),
        cost_estimate=cost(0, 12 * m * rc * width),
        name="pack",
    )(*parts)


def grad_kernel(cent_ref, col_ref, embed, *refs):
    *row_refs, out_ref, scale = refs
    m, _, rc, _ = embed.shape
    i = pl.program_id(0)
    for v in range(2):
        scale[v] = spread(col_ref[v, pl.ds(i, 1), :])
    total = jnp.zeros(out_ref.shape, F32)
    for j in range(m):
        es = []
        for v in range(2):
            s = lax.dot_general(cent_ref[...], embed[j, v], NT, preferred_element_type=F32)
            es.append(jnp.exp2(s * SOFT))
        for v in range(2):
            o = 1 - v
            c = jnp.concatenate([scale[o]] * (rc // 128), axis=1)
            r = slice(j % 2 * rc, (j % 2 + 1) * rc)
            codes = es[o] * es[o] * (GRAD / row_refs[j // 2][o : o + 1, r]) * c
            g = (es[v] * (GRAD / row_refs[j // 2][2 + v : 3 + v, r]) - codes).astype(BF16)
            total = total + jnp.dot(g, embed[j, v], preferred_element_type=F32)
    out_ref[...] = total


def grad_pass(centers, embeds, row, col):
    protos, width = centers.shape
    m, _, rc, _ = embeds.shape
    kt = tile_of(protos, 512)
    n = protos // kt
    whole = lambda *s: pl.BlockSpec(s, lambda i: (0,) * len(s))
    return pl.pallas_call(
        grad_kernel,
        grid=(n,),
        in_specs=[
            pl.BlockSpec((kt, width), lambda i: (i, 0)),
            whole(2, n, kt),
            whole(m, 2, rc, width),
        ]
        + [whole(4, 2 * rc)] * (m // 2),
        out_specs=pl.BlockSpec((kt, width), lambda i: (i, 0)),
        out_shape=jax.ShapeDtypeStruct((protos, width), F32),
        scratch_shapes=[pltpu.VMEM((2, kt, 128), F32)],
        compiler_params=params(48),
        cost_estimate=cost(8 * protos * m * rc * width, 4 * m * rc * width),
        name="grad_pass",
    )(centers, col.reshape(2, n, kt), embeds, *row)


def place_kernel(at_ref, *refs):
    m = len(refs) - 2
    out_ref, sems = refs[m], refs[m + 1]
    copies = []
    for j in range(m):
        size = refs[j].shape[0]
        where = pl.ds(pl.multiple_of(at_ref[j], 8), size)
        copies.append(pltpu.make_async_copy(refs[j], out_ref.at[where], sems.at[j]))
    for c in copies:
        c.start()
    for c in copies:
        c.wait()


def place(pieces, at, size):
    m = len(pieces)
    return pl.pallas_call(
        place_kernel,
        in_specs=[pl.BlockSpec(memory_space=pltpu.SMEM)]
        + [pl.BlockSpec(memory_space=pltpu.VMEM)] * m,
        out_specs=pl.BlockSpec(memory_space=pl.ANY),
        out_shape=jax.ShapeDtypeStruct((size, pieces[0].shape[1]), F32),
        scratch_shapes=[pltpu.SemaphoreType.DMA((m,))],
        compiler_params=params(24),
        name="place",
    )(jnp.stack(at).astype(jnp.int32), *pieces)


def swap(x, axis, n, m):
    return lax.ppermute(x, axis, [(i, i ^ m) for i in range(n)])


def col_exchange(x, n):
    if n > 1:
        x = x + swap(x, "batch", n, 1)
    m = 2
    while n // m > 4:
        x = x + swap(x, "batch", n, m)
        m *= 2
    return [x] + [swap(x, "batch", n, k * m) for k in range(1, n // m)]


def row_exchange(x, n):
    m = 1
    while m < n:
        x = x + swap(x, "proto", n, m)
        m *= 2
    return x


def gather_plan(n):
    bits = [2**j for j in range(1, n.bit_length()) if 2**j < n]
    plan, keys_a, keys_b = [], [0], [0]
    for m, w in zip(bits, bits[::-1]):
        plan += [((k, m), (q, w)) for k, q in zip(keys_a, keys_b)]
        keys_a, keys_b = keys_a + [k ^ m for k in keys_a], keys_b + [k ^ w for k in keys_b]
    return plan


def send_pair(have, pair, n):
    for h, (k, m) in zip(have, pair):
        h[k ^ m] = swap(h[k], "batch", n, m)


def gather_rows(x, n):
    return [x] + [swap(x, "batch", n, k) for k in range(2, n, 2)]


def norm_back(grad, given):
    x = given.astype(F32)
    inverse = lax.rsqrt(jnp.sum(x * x, axis=-1, keepdims=True) + 1e-06)
    unit = x * inverse
    return inverse * (grad - unit * jnp.sum(unit * grad, axis=-1, keepdims=True))


def cut(x, at, size):
    return lax.dynamic_slice_in_dim(x, at, size, axis=0)


def halve_over_proto(x, n, m=1):
    size = x.shape[0] // 2
    side = (lax.axis_index("proto") // m) % 2
    return cut(x, side * size, size), swap(cut(x, (1 - side) * size, size), "proto", n, m)


def home(i, n, size):
    at = 0 * i
    for m in bits_of(n):
        size //= 2
        at = at + (i // m) % 2 * size
    return at


def spread_out(pieces, n):
    bits = bits_of(n)[::-1]
    keys = [0, bits[0]]
    size = pieces[0].shape[0]
    x = jnp.concatenate(pieces, axis=0)
    for m in bits[1:-1]:
        x = jnp.concatenate([x, swap(x, "proto", n, m)], axis=0)
        keys = keys + [k ^ m for k in keys]
    y = swap(x, "proto", n, bits[-1])
    found = {}
    for j, k in enumerate(keys):
        found[k] = x[j * size : (j + 1) * size]
        found[k ^ bits[-1]] = y[j * size : (j + 1) * size]
    return found


def bits_of(n):
    return [2**j for j in range(n.bit_length()) if 2**j < n]


def shard_back(pair, given, n):
    x = pair[0] + pair[1]
    for m in bits_of(n)[2:]:
        a, b = halve_over_proto(x, n, m)
        x = a + b
    at = home(lax.axis_index("proto"), n, given.shape[0])
    return norm_back(x, cut(given, at, x.shape[0]))


def per_device(nb, npr, features, prototypes):
    _, rows, width = features.shape
    protos = prototypes.shape[0]
    me = lax.axis_index("batch")
    chip, core = me // 2, me % 2
    share = protos // (nb // 2)

    (lo, hi, centers, col, tot, soft), base = first(features, prototypes)
    parts = col_exchange(col, nb)
    have, plan = [{0: lo}, {0: hi}], gather_plan(nb)
    have, parts = lax.optimization_barrier((have, parts))
    for step in range(ITERS - 1):
        if plan:
            send_pair(have, plan.pop(0), nb)
        (row,) = row_pass(base, parts)
        if step == 0:
            both = row_exchange(jnp.concatenate([row, tot]), npr)
            row, tot = both[:2], both[2:]
        else:
            row = row_exchange(row, npr)
        col = col_pass(base, row)
        col, have = lax.optimization_barrier((col, have))
        parts = col_exchange(col, nb)
        have, parts = lax.optimization_barrier((have, parts))
    for pair in plan:
        send_pair(have, pair, nb)
    row, code = row_pass(base, parts, centers)
    row = row_exchange(row, npr)
    row, have = lax.optimization_barrier((row, have))
    rows_all = gather_rows(jnp.concatenate([row, tot]), nb)
    embeds = pack([have[h][k] for k in range(0, nb, 2) for h in range(2)])
    col = (1.0 / sum(parts)).reshape(2, protos)
    half = share // 2
    quarter = half // 2

    def grads(at):
        c = lax.dynamic_slice_in_dim(col, at, half, axis=1)
        return grad_pass(cut(centers, at, half), embeds, rows_all, c)

    gf = [
        soft[v] * (GRAD / tot[v])[:, None] - code[1 - v] * (GRAD / row[1 - v])[:, None]
        for v in range(2)
    ]
    pair = halve_over_proto(gf[0], npr, 1)
    theirs = grads(chip * share + (1 - core) * half)
    theirs, pair, late = lax.optimization_barrier((theirs, pair, gf[1]))
    theirs = swap(theirs, "batch", nb, 1)
    pair = halve_over_proto(pair[0] + pair[1], npr, 2)
    pair_late = halve_over_proto(late, npr, 1)
    mine = grads(chip * share + core * half)
    mine, theirs, pair, pair_late = lax.optimization_barrier((mine, theirs, pair, pair_late))
    grad = norm_back(mine + theirs, cut(prototypes, chip * share + core * half, half))

    have, plan = [{0: grad[:quarter]}, {0: grad[quarter:]}], gather_plan(nb)
    last = bits_of(npr)[-1]
    send_pair(have, plan.pop(0), nb)
    shard = shard_back(pair, features[0], npr)
    near = swap(shard, "proto", npr, last)
    late = halve_over_proto(pair_late[0] + pair_late[1], npr, 2)
    have, near, late = lax.optimization_barrier((have, near, late))
    send_pair(have, plan.pop(0), nb)
    shards = [spread_out([shard, near], npr), shard_back(late, features[1], npr)]
    near = swap(shards[1], "proto", npr, last)
    have, near, first_view = lax.optimization_barrier((have, near, shards[0]))
    for p in plan:
        send_pair(have, p, nb)
    shards = [first_view, spread_out([shards[1], near], npr)]
    idx = lax.axis_index("proto")
    out, where = [], []
    for v in range(2):
        for k, x in shards[v].items():
            out.append(x)
            where.append(home(idx ^ k, npr, rows) + v * rows)
    grad_features = place(out, where, 2 * rows).reshape(2, rows, width)

    out, where = [], []
    for k in have[0]:
        for h in range(2):
            at = (chip ^ (k // 2)) * share + h * quarter
            out += [have[h][k], swap(have[h][k], "batch", nb, 1)]
            where += [at + core * half, at + (1 - core) * half]
    return grad_features, place(out, where, protos)


def solution(mesh):
    nb, npr = mesh.shape["batch"], mesh.shape["proto"]
    return jax.shard_map(
        lambda f, p: per_device(nb, npr, f, p),
        mesh=mesh,
        in_specs=(P(None, "batch", None), P("proto", None)),
        out_specs=(P(None, "batch", None), P("proto", None)),
        check_vma=False,
    )
```

```python
import jax
import jax.numpy as jnp
from jax import lax
from jax.experimental import pallas as pl
from jax.experimental.pallas import tpu as pltpu
from jax.sharding import PartitionSpec as P

ITERS = 3
LOG2E = 1.4426950408889634
SOFT = 10.0 * LOG2E
GRAD = 5.0
F32 = jnp.float32
BF16 = jnp.bfloat16
NT = (((1,), (1,)), ((), ()))


def tile_of(n, most):
    t = most
    while n % t:
        t //= 2
    return t


def params(mib):
    return pltpu.CompilerParams(vmem_limit_bytes=mib * 2**20)


def cost(flops, nbytes):
    return pl.CostEstimate(flops=flops, bytes_accessed=nbytes, transcendentals=0)


def lane_fold(x):
    total = x[:, :128]
    for j in range(1, x.shape[1] // 128):
        total = total + x[:, 128 * j : 128 * (j + 1)]
    return total


def sub_fold(x):
    total = x[:8]
    for j in range(1, x.shape[0] // 8):
        total = total + x[8 * j : 8 * (j + 1)]
    return total


def spread(row):
    return jnp.broadcast_to(row, (128, row.shape[1])).T


def unit_of(x):
    inv = lax.rsqrt(jnp.sum(x * x, axis=-1, keepdims=True) + 1e-06)
    return x * inv, inv


def two_terms(x):
    high = x.astype(BF16)
    return high, (x - high.astype(F32)).astype(BF16)


def in_hbm(x):
    return pltpu.with_memory_space_constraint(x, pltpu.HBM)


def in_vmem():
    return pl.BlockSpec(memory_space=pltpu.VMEM)


def first_kernel(feat_ref, proto_ref, lo_ref, hi_ref, cent_ref, col_ref, tot_ref, soft_ref, *refs):
    kept_ref, *base_refs, acc, embed_ref, sems = refs
    i = pl.program_id(0)
    rows = feat_ref.shape[1]
    kt = proto_ref.shape[0]
    rc = base_refs[0].shape[1]

    @pl.when(i == 0)
    def _():
        acc[...] = jnp.zeros_like(acc)
        soft_ref[...] = jnp.zeros_like(soft_ref)
        for v in range(2):
            e = unit_of(feat_ref[v].astype(F32))[0].astype(BF16)
            embed_ref[v] = e
            lo_ref[v] = e[: rows // 2].astype(F32)
            hi_ref[v] = e[rows // 2 :].astype(F32)

    cent_ref[...] = unit_of(proto_ref[...].astype(F32))[0].astype(BF16)
    for v in range(2):
        col = jnp.zeros((8, kt), F32)
        for j in range(rows // rc):
            r = slice(j * rc, (j + 1) * rc)
            s = lax.dot_general(embed_ref[v, r, :], cent_ref[...], NT, preferred_element_type=F32)
            e = jnp.exp2(s * SOFT)
            acc[v, r, :] += lane_fold(e)
            soft_ref[v, r, :] += jnp.dot(e.astype(BF16), cent_ref[...], preferred_element_type=F32)
            b = e * e
            base_refs[v * (rows // rc) + j][i] = b.astype(BF16)
            col = col + sub_fold(b)
        col_ref[v, pl.ds(i, 1), :] = jnp.sum(col, axis=0, keepdims=True)

    def keep(tile, j):
        return pltpu.make_async_copy(base_refs[j].at[tile], kept_ref.at[j, tile], sems.at[tile, j])

    for j in range(len(base_refs)):
        keep(i, j).start()

    @pl.when(i == pl.num_programs(0) - 1)
    def _():
        for tile in range(sems.shape[0]):
            for j in range(len(base_refs)):
                keep(tile, j).wait()
        for v in range(2):
            tot_ref[v : v + 1, :] = jnp.sum(acc[v].T, axis=0, keepdims=True)


def first(features, prototypes):
    _, rows, width = features.shape
    protos = prototypes.shape[0]
    kt = tile_of(protos, 1024)
    n = protos // kt
    rc = tile_of(rows, 256)
    m = 2 * rows // rc
    outs = pl.pallas_call(
        first_kernel,
        grid=(n,),
        in_specs=[in_vmem(), pl.BlockSpec((kt, width), lambda i: (i, 0))],
        out_specs=[
            in_vmem(),
            in_vmem(),
            pl.BlockSpec((kt, width), lambda i: (i, 0)),
            in_vmem(),
            in_vmem(),
            in_vmem(),
            pl.BlockSpec(memory_space=pl.ANY),
        ]
        + [in_vmem()] * m,
        out_shape=[
            jax.ShapeDtypeStruct((2, rows // 2, width), F32),
            jax.ShapeDtypeStruct((2, rows // 2, width), F32),
            jax.ShapeDtypeStruct((protos, width), BF16),
            jax.ShapeDtypeStruct((2, n, kt), F32),
            jax.ShapeDtypeStruct((2, rows), F32),
            jax.ShapeDtypeStruct((2, rows, width), F32),
            pltpu.HBM((m, n, rc, kt), BF16),
        ]
        + [pltpu.VMEM((n, rc, kt), BF16)] * m,
        scratch_shapes=[
            pltpu.VMEM((2, rows, 128), F32),
            pltpu.VMEM((2, rows, width), BF16),
            pltpu.SemaphoreType.DMA((n, m)),
        ],
        compiler_params=params(16),
        cost_estimate=cost(16 * rows * protos * width, 0),
        name="first",
    )(features, prototypes)
    return outs[:7], outs[7:]


def load_scales(part_refs, rows_ref, cols_ref, v):
    n, kt = rows_ref.shape
    half = kt // 2
    for i in range(n):
        c = 1.0 / sum(p[v, i : i + 1, :] for p in part_refs)
        rows_ref[i : i + 1, :] = c
        high, low = two_terms(c[:, half:])
        cols_ref[i] = jnp.concatenate([high, low, jnp.zeros((126, half), BF16)], axis=0).T


def block_sum(base_ref, rows_ref, cols_ref, acc):
    n, rc, kt = base_ref.shape
    half = kt // 2
    total = jnp.dot(base_ref[0, :, half:], cols_ref[0], preferred_element_type=F32)
    for i in range(1, n):
        total = total + jnp.dot(base_ref[i, :, half:], cols_ref[i], preferred_element_type=F32)
    acc[...] = total
    step = 32
    for j in range(0, rc, step):
        r = slice(j, j + step)
        part = acc[r]
        for i in range(n):
            part = part + lane_fold(base_ref[i, r, :half].astype(F32) * rows_ref[i : i + 1, :half])
        acc[r] = part
    return jnp.sum(acc[...].T, axis=0, keepdims=True)


def row_kernel(m, *refs):
    base_refs, part_refs = refs[:m], refs[m:-4]
    out_ref, rows_ref, cols_ref, acc = refs[-4:]
    rc = base_refs[0].shape[1]
    for v in range(2):
        load_scales(part_refs, rows_ref, cols_ref, v)
        for j in range(m // 2):
            sums = block_sum(base_refs[v * (m // 2) + j], rows_ref, cols_ref, acc)
            out_ref[v : v + 1, j * rc : (j + 1) * rc] = sums


def row_pass(base, parts):
    m = len(base)
    n, rc, kt = base[0].shape
    rows = m // 2 * rc
    return pl.pallas_call(
        lambda *refs: row_kernel(m, *refs),
        in_specs=[in_vmem()] * (m + len(parts)),
        out_specs=in_vmem(),
        out_shape=jax.ShapeDtypeStruct((2, rows), F32),
        scratch_shapes=[
            pltpu.VMEM((n, kt), F32),
            pltpu.VMEM((n, kt // 2, 128), BF16),
            pltpu.VMEM((rc, 128), F32),
        ],
        compiler_params=params(16),
        cost_estimate=cost(0, 4 * n * rows * kt),
        name="row_pass",
    )(*base, *parts)


def row_last_kernel(base_ref, *refs):
    *part_refs, out_ref, acc = refs
    m, _, rc, kt = base_ref.shape
    half = kt // 2
    i = pl.program_id(0)

    @pl.when(i == 0)
    def _():
        acc[...] = jnp.zeros_like(acc)

    for v in range(2):
        c = 1.0 / sum(p[v, pl.ds(i, 1), :] for p in part_refs)
        high, low = two_terms(c[:, half:])
        cols = jnp.concatenate([high, low, jnp.zeros((126, half), BF16)], axis=0).T
        for j in range(m // 2):
            k = v * (m // 2) + j
            total = jnp.dot(base_ref[k, 0, :, half:], cols, preferred_element_type=F32)
            total = total + lane_fold(base_ref[k, 0, :, :half].astype(F32) * c[:, :half])
            acc[v, j * rc : (j + 1) * rc, :] += total

    @pl.when(i == pl.num_programs(0) - 1)
    def _():
        for v in range(2):
            out_ref[v : v + 1, :] = jnp.sum(acc[v].T, axis=0, keepdims=True)


def row_last(kept, parts):
    m, n, rc, kt = kept.shape
    rows = m // 2 * rc
    return pl.pallas_call(
        row_last_kernel,
        grid=(n,),
        in_specs=[pl.BlockSpec((m, 1, rc, kt), lambda i: (0, i, 0, 0))] + [in_vmem()] * len(parts),
        out_specs=in_vmem(),
        out_shape=jax.ShapeDtypeStruct((2, rows), F32),
        scratch_shapes=[pltpu.VMEM((2, rows, 128), F32)],
        compiler_params=params(16),
        cost_estimate=cost(0, 4 * n * rows * kt),
        name="row_last",
    )(in_hbm(kept), *parts)


def code_kernel(v, cent_ref, base_ref, *refs):
    *part_refs, out_ref = refs
    m, _, rc, _ = base_ref.shape
    i = pl.program_id(0)

    @pl.when(i == 0)
    def _():
        out_ref[...] = jnp.zeros_like(out_ref)

    c = spread(1.0 / sum(p[v, pl.ds(i, 1), :] for p in part_refs))
    c = jnp.concatenate([c] * (cent_ref.shape[1] // 128), axis=1)
    scaled = (cent_ref[...].astype(F32) * c).astype(BF16)
    for j in range(m):
        r = slice(j * rc, (j + 1) * rc)
        out_ref[r, :] += jnp.dot(base_ref[j, 0], scaled, preferred_element_type=F32)


def code_pass(kept, centers, parts, v):
    m, n, rc, kt = kept.shape
    m //= 2
    width = centers.shape[1]
    return pl.pallas_call(
        lambda *refs: code_kernel(v, *refs),
        grid=(n,),
        in_specs=[
            pl.BlockSpec((kt, width), lambda i: (i, 0)),
            pl.BlockSpec((m, 1, rc, kt), lambda i: (v, i, 0, 0)),
        ]
        + [in_vmem()] * len(parts),
        out_specs=in_vmem(),
        out_shape=jax.ShapeDtypeStruct((m * rc, width), F32),
        compiler_params=params(16),
        cost_estimate=cost(2 * n * m * rc * kt * width, 0),
        name="code_pass",
    )(in_hbm(centers), in_hbm(kept), *parts)


def col_kernel(total_ref, *refs):
    *base_refs, out_ref = refs
    m = len(base_refs) // 2
    n, rc, kt = base_refs[0].shape
    for v in range(2):
        high, low = two_terms(1.0 / total_ref[v : v + 1, :])
        r = jnp.concatenate([high, low, jnp.zeros((14, m * rc), BF16)], axis=0)
        for i in range(n):
            total = jnp.zeros((16, kt), F32)
            for j in range(m):
                total = total + jnp.dot(
                    r[:, j * rc : (j + 1) * rc],
                    base_refs[v * m + j][i],
                    preferred_element_type=F32,
                )
            out_ref[v, i : i + 1, :] = total[0:1] + total[1:2]


def col_pass(base, total):
    n, rc, kt = base[0].shape
    m = len(base)
    return pl.pallas_call(
        col_kernel,
        in_specs=[in_vmem()] * (m + 1),
        out_specs=in_vmem(),
        out_shape=jax.ShapeDtypeStruct((2, n, kt), F32),
        compiler_params=params(16),
        cost_estimate=cost(0, 4 * n * m // 2 * rc * kt),
        name="col_pass",
    )(total, *base)


def pack_kernel(*refs):
    *part_refs, out_ref = refs
    for j, p in enumerate(part_refs):
        out_ref[j] = p[...].astype(BF16)


def pack(parts):
    _, rc, width = parts[0].shape
    m = len(parts)
    return pl.pallas_call(
        pack_kernel,
        grid=(2,),
        in_specs=[pl.BlockSpec((1, rc, width), lambda v: (v, 0, 0))] * m,
        out_specs=pl.BlockSpec((m, 1, rc, width), lambda v: (0, v, 0, 0)),
        out_shape=jax.ShapeDtypeStruct((m, 2, rc, width), BF16),
        compiler_params=params(16),
        cost_estimate=cost(0, 12 * m * rc * width),
        name="pack",
    )(*parts)


def grad_kernel(cent_ref, col_ref, embed, *refs):
    *row_refs, out_ref, scale = refs
    m, _, rc, _ = embed.shape
    i = pl.program_id(0)
    for v in range(2):
        scale[v] = spread(col_ref[v, pl.ds(i, 1), :])
    total = jnp.zeros(out_ref.shape, F32)
    for j in range(m):
        es = []
        for v in range(2):
            s = lax.dot_general(cent_ref[...], embed[j, v], NT, preferred_element_type=F32)
            es.append(jnp.exp2(s * SOFT))
        for v in range(2):
            o = 1 - v
            c = jnp.concatenate([scale[o]] * (rc // 128), axis=1)
            r = slice(j % 2 * rc, (j % 2 + 1) * rc)
            codes = es[o] * es[o] * (GRAD / row_refs[j // 2][o : o + 1, r]) * c
            g = (es[v] * (GRAD / row_refs[j // 2][2 + v : 3 + v, r]) - codes).astype(BF16)
            total = total + jnp.dot(g, embed[j, v], preferred_element_type=F32)
    out_ref[...] = total


def grad_pass(centers, embeds, row, col):
    protos, width = centers.shape
    m, _, rc, _ = embeds.shape
    kt = tile_of(protos, 512)
    n = protos // kt
    whole = lambda *s: pl.BlockSpec(s, lambda i: (0,) * len(s))
    return pl.pallas_call(
        grad_kernel,
        grid=(n,),
        in_specs=[
            pl.BlockSpec((kt, width), lambda i: (i, 0)),
            in_vmem(),
            in_vmem(),
        ]
        + [in_vmem()] * (m // 2),
        out_specs=pl.BlockSpec((kt, width), lambda i: (i, 0)),
        out_shape=jax.ShapeDtypeStruct((protos, width), F32),
        scratch_shapes=[pltpu.VMEM((2, kt, 128), F32)],
        compiler_params=params(16),
        cost_estimate=cost(8 * protos * m * rc * width, 4 * m * rc * width),
        name="grad_pass",
    )(centers, col.reshape(2, n, kt), embeds, *row)


def place_kernel(at_ref, *refs):
    m = len(refs) - 2
    out_ref, sems = refs[m], refs[m + 1]
    copies = []
    for j in range(m):
        size = refs[j].shape[0]
        where = pl.ds(pl.multiple_of(at_ref[j], 8), size)
        copies.append(pltpu.make_async_copy(refs[j], out_ref.at[where], sems.at[j]))
    for c in copies:
        c.start()
    for c in copies:
        c.wait()


def place(pieces, at, size):
    m = len(pieces)
    return pl.pallas_call(
        place_kernel,
        in_specs=[pl.BlockSpec(memory_space=pltpu.SMEM)]
        + [pl.BlockSpec(memory_space=pltpu.VMEM)] * m,
        out_specs=pl.BlockSpec(memory_space=pl.ANY),
        out_shape=jax.ShapeDtypeStruct((size, pieces[0].shape[1]), F32),
        scratch_shapes=[pltpu.SemaphoreType.DMA((m,))],
        compiler_params=params(16),
        name="place",
    )(jnp.stack(at).astype(jnp.int32), *pieces)


def swap(x, axis, n, m):
    return lax.ppermute(x, axis, [(i, i ^ m) for i in range(n)])


def col_exchange(x, n):
    if n > 1:
        x = x + swap(x, "batch", n, 1)
    m = 2
    while n // m > 4:
        x = x + swap(x, "batch", n, m)
        m *= 2
    return [x] + [swap(x, "batch", n, k * m) for k in range(1, n // m)]


def row_exchange(x, n):
    m = 1
    while m < n:
        x = x + swap(x, "proto", n, m)
        m *= 2
    return x


def gather_plan(n):
    bits = [2**j for j in range(1, n.bit_length()) if 2**j < n]
    plan, keys_a, keys_b = [], [0], [0]
    for m, w in zip(bits, bits[::-1]):
        plan += [((k, m), (q, w)) for k, q in zip(keys_a, keys_b)]
        keys_a, keys_b = keys_a + [k ^ m for k in keys_a], keys_b + [k ^ w for k in keys_b]
    return plan


def send_pair(have, pair, n):
    for h, (k, m) in zip(have, pair):
        h[k ^ m] = swap(h[k], "batch", n, m)


def gather_rows(x, n):
    return [x] + [swap(x, "batch", n, k) for k in range(2, n, 2)]


def norm_back(grad, given):
    x = given.astype(F32)
    inverse = lax.rsqrt(jnp.sum(x * x, axis=-1, keepdims=True) + 1e-06)
    unit = x * inverse
    return inverse * (grad - unit * jnp.sum(unit * grad, axis=-1, keepdims=True))


def cut(x, at, size):
    return lax.dynamic_slice_in_dim(x, at, size, axis=0)


def tie(*xs):
    return lax.optimization_barrier(xs)


def per_device(nb, npr, features, prototypes):
    _, rows, width = features.shape
    protos = prototypes.shape[0]
    me = lax.axis_index("batch")
    chip, core = me // 2, me % 2
    share = protos // (nb // 2)

    (lo, hi, centers, col, tot, soft, kept), base = first(features, prototypes)
    parts = col_exchange(col, nb)
    have, plan = [{0: lo}, {0: hi}], gather_plan(nb)
    have, parts = lax.optimization_barrier((have, parts))
    for step in range(ITERS - 1):
        if plan:
            send_pair(have, plan.pop(0), nb)
        row = row_pass(base, parts)
        if step == 0:
            both = row_exchange(jnp.concatenate([row, tot]), npr)
            row, tot = both[:2], both[2:]
        else:
            row = row_exchange(row, npr)
        col = col_pass(base, row)
        col, have = lax.optimization_barrier((col, have))
        parts = col_exchange(col, nb)
        have, parts = lax.optimization_barrier((have, parts))
    for pair in plan:
        send_pair(have, pair, nb)
    row = row_exchange(row_last(kept, parts), npr)
    code = [code_pass(kept, centers, parts, v) for v in range(2)]
    row, have, centers, code, parts = tie(row, have, centers, code, parts)
    rows_all = gather_rows(jnp.concatenate([row, tot]), nb)
    embeds = pack([have[h][k] for k in range(0, nb, 2) for h in range(2)])
    col = (1.0 / sum(parts)).reshape(2, protos)
    half = share // 2
    quarter = half // 2

    def grads(at):
        c = lax.dynamic_slice_in_dim(col, at, quarter, axis=1)
        return grad_pass(cut(centers, at, quarter), embeds, rows_all, c)

    h = rows // 2
    d = []
    for v in range(2):
        part = soft[v] * (GRAD / tot[v])[:, None] - code[1 - v] * (GRAD / row[1 - v])[:, None]
        d += [part[:h], part[h:]]
    line = npr == 4
    if not line:
        d = [row_exchange(x, npr) for x in d]

    def hop(x, pairs):
        return lax.ppermute(x, "proto", pairs) if line else jnp.zeros_like(x)

    def inwards(x):
        return hop(x, [(0, 1), (3, 2)])

    def across(x):
        return hop(x, [(1, 2), (2, 1)])

    def outwards(x):
        return hop(x, [(1, 0), (2, 3)])

    mine_at = chip * share + core * half
    their_at = chip * share + (1 - core) * half
    plan = gather_plan(nb)

    def send(hs, k, m):
        got[hs][k ^ m] = swap(got[hs][k], "batch", nb, m)

    a0 = inwards(d[0])
    theirs = swap(grads(their_at), "batch", nb, 1)
    mine = grads(mine_at)
    mine, theirs, a0, d, features, prototypes = tie(mine, theirs, a0, d, features, prototypes)

    got = [{0: norm_back(mine + theirs, cut(prototypes, mine_at, quarter))}, {}]
    send(0, *plan[0][0])
    s0 = d[0] + a0
    a1, b0 = inwards(d[1]), across(s0)
    theirs = swap(grads(their_at + quarter), "batch", nb, 1)
    mine = grads(mine_at + quarter)
    mine, theirs, a1, b0, got, d = tie(mine, theirs, a1, b0, got, d)

    got[1][0] = norm_back(mine + theirs, cut(prototypes, mine_at + quarter, quarter))
    send(1, *plan[0][1])
    send(1, *plan[1][1])
    t0, s1 = s0 + b0, d[1] + a1
    a2, b1, c0 = inwards(d[2]), across(s1), outwards(t0)
    a2, b1, c0, got, d = tie(a2, b1, c0, got, d)

    send(0, *plan[1][0])
    for pair in plan[2:]:
        for hs in range(2):
            send(hs, *pair[hs])
    early = [(0, 0), (1, 0), (0, plan[0][0][1]), (1, plan[0][1][1])]
    near = {(hs, k): swap(got[hs][k], "batch", nb, 1) for hs, k in early}
    t1, s2 = s1 + b1, d[2] + a2
    a3, b2, c1 = inwards(d[3]), across(s2), outwards(t1)
    a3, b2, c1, got, near = tie(a3, b2, c1, got, near)

    t2, s3 = s2 + b2, d[3] + a3
    b3, c2 = across(s3), outwards(t2)
    out, where = [], []
    for k in got[0]:
        for hs in range(2):
            at = (chip ^ (k // 2)) * share + hs * quarter
            other = near[hs, k] if (hs, k) in near else swap(got[hs][k], "batch", nb, 1)
            out += [got[hs][k], other]
            where += [at + core * half, at + (1 - core) * half]
    out, b3, c2 = tie(out, b3, c2)
    t3 = s3 + b3
    c3 = outwards(t3)
    grad_prototypes = place(out, where, protos)
    grad_prototypes, c3 = tie(grad_prototypes, c3)

    z = lax.axis_index("proto")
    ends = jnp.logical_and(line, jnp.logical_or(z == 0, z == 3))
    chunks = [jnp.where(ends, c, t) for t, c in ((t0, c0), (t1, c1), (t2, c2), (t3, c3))]
    grad_embed = jnp.concatenate(chunks).reshape(2, rows, width)
    return norm_back(grad_embed, features), grad_prototypes


def solution(mesh):
    nb, npr = mesh.shape["batch"], mesh.shape["proto"]
    return jax.shard_map(
        lambda f, p: per_device(nb, npr, f, p),
        mesh=mesh,
        in_specs=(P(None, "batch", None), P("proto", None)),
        out_specs=(P(None, "batch", None), P("proto", None)),
        check_vma=False,
    )
```

```python
import jax
import jax.numpy as jnp
from jax import lax
from jax.experimental import pallas as pl
from jax.experimental.pallas import tpu as pltpu
from jax.sharding import PartitionSpec as P

ITERS = 3
LOG2E = 1.4426950408889634
SOFT = 10.0 * LOG2E
GRAD = 5.0
F32 = jnp.float32
BF16 = jnp.bfloat16
NT = (((1,), (1,)), ((), ()))


def tile_of(n, most):
    t = most
    while n % t:
        t //= 2
    return t


def params(mib):
    return pltpu.CompilerParams(vmem_limit_bytes=mib * 2**20)


def cost(flops, nbytes):
    return pl.CostEstimate(flops=flops, bytes_accessed=nbytes, transcendentals=0)


def lane_fold(x):
    total = x[:, :128]
    for j in range(1, x.shape[1] // 128):
        total = total + x[:, 128 * j : 128 * (j + 1)]
    return total


def sub_fold(x):
    total = x[:8]
    for j in range(1, x.shape[0] // 8):
        total = total + x[8 * j : 8 * (j + 1)]
    return total


def spread(row):
    return jnp.broadcast_to(row, (128, row.shape[1])).T


def unit_of(x):
    inv = lax.rsqrt(jnp.sum(x * x, axis=-1, keepdims=True) + 1e-06)
    return x * inv, inv


def two_terms(x):
    high = x.astype(BF16)
    return high, (x - high.astype(F32)).astype(BF16)


def in_hbm(x):
    return pltpu.with_memory_space_constraint(x, pltpu.HBM)


def in_vmem():
    return pl.BlockSpec(memory_space=pltpu.VMEM)


def first_kernel(feat_ref, proto_ref, lo_ref, hi_ref, cent_ref, col_ref, tot_ref, soft_ref, *refs):
    kept_ref, *base_refs, acc, embed_ref, sems = refs
    i = pl.program_id(0)
    rows = feat_ref.shape[1]
    kt = proto_ref.shape[0]
    rc = base_refs[0].shape[1]

    @pl.when(i == 0)
    def _():
        acc[...] = jnp.zeros_like(acc)
        soft_ref[...] = jnp.zeros_like(soft_ref)
        for v in range(2):
            e = unit_of(feat_ref[v].astype(F32))[0].astype(BF16)
            embed_ref[v] = e
            lo_ref[v] = e[: rows // 2].astype(F32)
            hi_ref[v] = e[rows // 2 :].astype(F32)

    cent_ref[...] = unit_of(proto_ref[...].astype(F32))[0].astype(BF16)
    for v in range(2):
        col = jnp.zeros((8, kt), F32)
        for j in range(rows // rc):
            r = slice(j * rc, (j + 1) * rc)
            s = lax.dot_general(embed_ref[v, r, :], cent_ref[...], NT, preferred_element_type=F32)
            e = jnp.exp2(s * SOFT)
            acc[v, r, :] += lane_fold(e)
            soft_ref[v, r, :] += jnp.dot(e.astype(BF16), cent_ref[...], preferred_element_type=F32)
            b = e * e
            base_refs[v * (rows // rc) + j][i] = b.astype(BF16)
            col = col + sub_fold(b)
        col_ref[v, pl.ds(i, 1), :] = jnp.sum(col, axis=0, keepdims=True)

    def keep(tile, j):
        return pltpu.make_async_copy(base_refs[j].at[tile], kept_ref.at[j, tile], sems.at[tile, j])

    for j in range(len(base_refs)):
        keep(i, j).start()

    @pl.when(i == pl.num_programs(0) - 1)
    def _():
        for tile in range(sems.shape[0]):
            for j in range(len(base_refs)):
                keep(tile, j).wait()
        for v in range(2):
            tot_ref[v : v + 1, :] = jnp.sum(acc[v].T, axis=0, keepdims=True)


def first(features, prototypes):
    _, rows, width = features.shape
    protos = prototypes.shape[0]
    kt = tile_of(protos, 1024)
    n = protos // kt
    rc = tile_of(rows, 256)
    m = 2 * rows // rc
    outs = pl.pallas_call(
        first_kernel,
        grid=(n,),
        in_specs=[in_vmem(), pl.BlockSpec((kt, width), lambda i: (i, 0))],
        out_specs=[
            in_vmem(),
            in_vmem(),
            pl.BlockSpec((kt, width), lambda i: (i, 0)),
            in_vmem(),
            in_vmem(),
            in_vmem(),
            pl.BlockSpec(memory_space=pl.ANY),
        ]
        + [in_vmem()] * m,
        out_shape=[
            jax.ShapeDtypeStruct((2, rows // 2, width), F32),
            jax.ShapeDtypeStruct((2, rows // 2, width), F32),
            jax.ShapeDtypeStruct((protos, width), BF16),
            jax.ShapeDtypeStruct((2, n, kt), F32),
            jax.ShapeDtypeStruct((2, rows), F32),
            jax.ShapeDtypeStruct((2, rows, width), F32),
            pltpu.HBM((m, n, rc, kt), BF16),
        ]
        + [pltpu.VMEM((n, rc, kt), BF16)] * m,
        scratch_shapes=[
            pltpu.VMEM((2, rows, 128), F32),
            pltpu.VMEM((2, rows, width), BF16),
            pltpu.SemaphoreType.DMA((n, m)),
        ],
        compiler_params=params(16),
        cost_estimate=cost(16 * rows * protos * width, 0),
        name="first",
    )(features, prototypes)
    return outs[:7], outs[7:]


def load_scales(part_refs, rows_ref, cols_ref, v):
    n, kt = rows_ref.shape
    half = kt // 2
    for i in range(n):
        c = 1.0 / sum(p[v, i : i + 1, :] for p in part_refs)
        rows_ref[i : i + 1, :] = c
        high, low = two_terms(c[:, half:])
        cols_ref[i] = jnp.concatenate([high, low, jnp.zeros((126, half), BF16)], axis=0).T


def block_sum(base_ref, rows_ref, cols_ref, acc):
    n, rc, kt = base_ref.shape
    half = kt // 2
    total = jnp.dot(base_ref[0, :, half:], cols_ref[0], preferred_element_type=F32)
    for i in range(1, n):
        total = total + jnp.dot(base_ref[i, :, half:], cols_ref[i], preferred_element_type=F32)
    acc[...] = total
    step = 32
    for j in range(0, rc, step):
        r = slice(j, j + step)
        part = acc[r]
        for i in range(n):
            part = part + lane_fold(base_ref[i, r, :half].astype(F32) * rows_ref[i : i + 1, :half])
        acc[r] = part
    return jnp.sum(acc[...].T, axis=0, keepdims=True)


def row_kernel(m, *refs):
    base_refs, part_refs = refs[:m], refs[m:-4]
    out_ref, rows_ref, cols_ref, acc = refs[-4:]
    rc = base_refs[0].shape[1]
    for v in range(2):
        load_scales(part_refs, rows_ref, cols_ref, v)
        for j in range(m // 2):
            sums = block_sum(base_refs[v * (m // 2) + j], rows_ref, cols_ref, acc)
            out_ref[v : v + 1, j * rc : (j + 1) * rc] = sums


def row_pass(base, parts):
    m = len(base)
    n, rc, kt = base[0].shape
    rows = m // 2 * rc
    return pl.pallas_call(
        lambda *refs: row_kernel(m, *refs),
        in_specs=[in_vmem()] * (m + len(parts)),
        out_specs=in_vmem(),
        out_shape=jax.ShapeDtypeStruct((2, rows), F32),
        scratch_shapes=[
            pltpu.VMEM((n, kt), F32),
            pltpu.VMEM((n, kt // 2, 128), BF16),
            pltpu.VMEM((rc, 128), F32),
        ],
        compiler_params=params(16),
        cost_estimate=cost(0, 4 * n * rows * kt),
        name="row_pass",
    )(*base, *parts)


def row_last_kernel(base_ref, cent_ref, *refs):
    *part_refs, out_ref, code_ref, acc = refs
    m, _, rc, _ = base_ref.shape
    i = pl.program_id(0)

    @pl.when(i == 0)
    def _():
        acc[...] = jnp.zeros_like(acc)
        code_ref[...] = jnp.zeros_like(code_ref)

    for v in range(2):
        c = 1.0 / sum(p[v, pl.ds(i, 1), :] for p in part_refs)
        for j in range(m // 2):
            r = slice(j * rc, (j + 1) * rc)
            w = base_ref[v * (m // 2) + j, 0].astype(F32) * c
            acc[v, r, :] += lane_fold(w)
            code_ref[v, r, :] += jnp.dot(w.astype(BF16), cent_ref[...], preferred_element_type=F32)

    @pl.when(i == pl.num_programs(0) - 1)
    def _():
        for v in range(2):
            out_ref[v : v + 1, :] = jnp.sum(acc[v].T, axis=0, keepdims=True)


def row_last(kept, centers, parts):
    m, n, rc, kt = kept.shape
    rows = m // 2 * rc
    width = centers.shape[1]
    return pl.pallas_call(
        row_last_kernel,
        grid=(n,),
        in_specs=[
            pl.BlockSpec((m, 1, rc, kt), lambda i: (0, i, 0, 0)),
            pl.BlockSpec((kt, width), lambda i: (i, 0)),
        ]
        + [in_vmem()] * len(parts),
        out_specs=[in_vmem()] * 2,
        out_shape=[
            jax.ShapeDtypeStruct((2, rows), F32),
            jax.ShapeDtypeStruct((2, rows, width), F32),
        ],
        scratch_shapes=[pltpu.VMEM((2, rows, 128), F32)],
        compiler_params=params(16),
        cost_estimate=cost(0, 8 * n * rows * kt),
        name="row_last",
    )(in_hbm(kept), in_hbm(centers), *parts)


def col_kernel(total_ref, *refs):
    *base_refs, out_ref = refs
    m = len(base_refs) // 2
    n, rc, kt = base_refs[0].shape
    for v in range(2):
        high, low = two_terms(1.0 / total_ref[v : v + 1, :])
        r = jnp.concatenate([high, low, jnp.zeros((14, m * rc), BF16)], axis=0)
        for i in range(n):
            total = jnp.zeros((16, kt), F32)
            for j in range(m):
                total = total + jnp.dot(
                    r[:, j * rc : (j + 1) * rc],
                    base_refs[v * m + j][i],
                    preferred_element_type=F32,
                )
            out_ref[v, i : i + 1, :] = total[0:1] + total[1:2]


def col_pass(base, total):
    n, rc, kt = base[0].shape
    m = len(base)
    return pl.pallas_call(
        col_kernel,
        in_specs=[in_vmem()] * (m + 1),
        out_specs=in_vmem(),
        out_shape=jax.ShapeDtypeStruct((2, n, kt), F32),
        compiler_params=params(16),
        cost_estimate=cost(0, 4 * n * m // 2 * rc * kt),
        name="col_pass",
    )(total, *base)


def pack_kernel(*refs):
    *part_refs, out_ref = refs
    for j, p in enumerate(part_refs):
        out_ref[j] = p[...].astype(BF16)


def pack(parts):
    _, rc, width = parts[0].shape
    m = len(parts)
    return pl.pallas_call(
        pack_kernel,
        grid=(2,),
        in_specs=[pl.BlockSpec((1, rc, width), lambda v: (v, 0, 0))] * m,
        out_specs=pl.BlockSpec((m, 1, rc, width), lambda v: (0, v, 0, 0)),
        out_shape=jax.ShapeDtypeStruct((m, 2, rc, width), BF16),
        compiler_params=params(32),
        cost_estimate=cost(0, 12 * m * rc * width),
        name="pack",
    )(*parts)


def grad_kernel(cent_ref, col_ref, embed, *refs):
    *row_refs, out_ref, scale = refs
    m, _, rc, _ = embed.shape
    i = pl.program_id(0)
    for v in range(2):
        scale[v] = spread(col_ref[v, pl.ds(i, 1), :])
    total = jnp.zeros(out_ref.shape, F32)
    for j in range(m):
        es = []
        for v in range(2):
            s = lax.dot_general(cent_ref[...], embed[j, v], NT, preferred_element_type=F32)
            es.append(jnp.exp2(s * SOFT))
        for v in range(2):
            o = 1 - v
            c = jnp.concatenate([scale[o]] * (rc // 128), axis=1)
            r = slice(j % 2 * rc, (j % 2 + 1) * rc)
            codes = es[o] * es[o] * (GRAD / row_refs[j // 2][o : o + 1, r]) * c
            g = (es[v] * (GRAD / row_refs[j // 2][2 + v : 3 + v, r]) - codes).astype(BF16)
            total = total + jnp.dot(g, embed[j, v], preferred_element_type=F32)
    out_ref[...] = total


def grad_pass(centers, embeds, row, col):
    protos, width = centers.shape
    m, _, rc, _ = embeds.shape
    kt = tile_of(protos, 512)
    n = protos // kt
    whole = lambda *s: pl.BlockSpec(s, lambda i: (0,) * len(s))
    return pl.pallas_call(
        grad_kernel,
        grid=(n,),
        in_specs=[
            pl.BlockSpec((kt, width), lambda i: (i, 0)),
            whole(2, n, kt),
            whole(m, 2, rc, width),
        ]
        + [whole(4, 2 * rc)] * (m // 2),
        out_specs=pl.BlockSpec((kt, width), lambda i: (i, 0)),
        out_shape=jax.ShapeDtypeStruct((protos, width), F32),
        scratch_shapes=[pltpu.VMEM((2, kt, 128), F32)],
        compiler_params=params(48),
        cost_estimate=cost(8 * protos * m * rc * width, 4 * m * rc * width),
        name="grad_pass",
    )(centers, col.reshape(2, n, kt), embeds, *row)


def place_kernel(at_ref, *refs):
    m = len(refs) - 2
    out_ref, sems = refs[m], refs[m + 1]
    copies = []
    for j in range(m):
        size = refs[j].shape[0]
        where = pl.ds(pl.multiple_of(at_ref[j], 8), size)
        copies.append(pltpu.make_async_copy(refs[j], out_ref.at[where], sems.at[j]))
    for c in copies:
        c.start()
    for c in copies:
        c.wait()


def place(pieces, at, size):
    m = len(pieces)
    return pl.pallas_call(
        place_kernel,
        in_specs=[pl.BlockSpec(memory_space=pltpu.SMEM)]
        + [pl.BlockSpec(memory_space=pltpu.VMEM)] * m,
        out_specs=pl.BlockSpec(memory_space=pl.ANY),
        out_shape=jax.ShapeDtypeStruct((size, pieces[0].shape[1]), F32),
        scratch_shapes=[pltpu.SemaphoreType.DMA((m,))],
        compiler_params=params(24),
        cost_estimate=cost(0, 12 * size * pieces[0].shape[1]),
        name="place",
    )(jnp.stack(at).astype(jnp.int32), *pieces)


def swap(x, axis, n, m):
    return lax.ppermute(x, axis, [(i, i ^ m) for i in range(n)])


def col_exchange(x, n):
    if n > 1:
        x = x + swap(x, "batch", n, 1)
    m = 2
    while n // m > 4:
        x = x + swap(x, "batch", n, m)
        m *= 2
    return [x] + [swap(x, "batch", n, k * m) for k in range(1, n // m)]


def row_exchange(x, n):
    m = 1
    while m < n:
        x = x + swap(x, "proto", n, m)
        m *= 2
    return x


def gather_plan(n):
    bits = [2**j for j in range(1, n.bit_length()) if 2**j < n]
    plan, keys_a, keys_b = [], [0], [0]
    for m, w in zip(bits, bits[::-1]):
        plan += [((k, m), (q, w)) for k, q in zip(keys_a, keys_b)]
        keys_a, keys_b = keys_a + [k ^ m for k in keys_a], keys_b + [k ^ w for k in keys_b]
    return plan


def send_pair(have, pair, n):
    for h, (k, m) in zip(have, pair):
        h[k ^ m] = swap(h[k], "batch", n, m)


def gather_rows(x, n):
    return [x] + [swap(x, "batch", n, k) for k in range(2, n, 2)]


def norm_back(grad, given):
    x = given.astype(F32)
    inverse = lax.rsqrt(jnp.sum(x * x, axis=-1, keepdims=True) + 1e-06)
    unit = x * inverse
    return inverse * (grad - unit * jnp.sum(unit * grad, axis=-1, keepdims=True))


def cut(x, at, size):
    return lax.dynamic_slice_in_dim(x, at, size, axis=0)


def halve_over_proto(x, n, m=1):
    size = x.shape[0] // 2
    side = (lax.axis_index("proto") // m) % 2
    return cut(x, side * size, size), swap(cut(x, (1 - side) * size, size), "proto", n, m)


def home(i, n, size):
    at = 0 * i
    for m in bits_of(n):
        size //= 2
        at = at + (i // m) % 2 * size
    return at


def spread_out(pieces, n):
    bits = bits_of(n)[::-1]
    keys = [0, bits[0]]
    size = pieces[0].shape[0]
    x = jnp.concatenate(pieces, axis=0)
    for m in bits[1:-1]:
        x = jnp.concatenate([x, swap(x, "proto", n, m)], axis=0)
        keys = keys + [k ^ m for k in keys]
    y = swap(x, "proto", n, bits[-1])
    found = {}
    for j, k in enumerate(keys):
        found[k] = x[j * size : (j + 1) * size]
        found[k ^ bits[-1]] = y[j * size : (j + 1) * size]
    return found


def bits_of(n):
    return [2**j for j in range(n.bit_length()) if 2**j < n]


def shard_back(pair, given, n):
    x = pair[0] + pair[1]
    for m in bits_of(n)[2:]:
        a, b = halve_over_proto(x, n, m)
        x = a + b
    at = home(lax.axis_index("proto"), n, given.shape[0])
    return norm_back(x, cut(given, at, x.shape[0]))


def per_device(nb, npr, features, prototypes):
    _, rows, width = features.shape
    protos = prototypes.shape[0]
    me = lax.axis_index("batch")
    chip, core = me // 2, me % 2
    share = protos // (nb // 2)

    (lo, hi, centers, col, tot, soft, kept), base = first(features, prototypes)
    parts = col_exchange(col, nb)
    have, plan = [{0: lo}, {0: hi}], gather_plan(nb)
    have, parts = lax.optimization_barrier((have, parts))
    for step in range(ITERS - 1):
        if plan:
            send_pair(have, plan.pop(0), nb)
        row = row_pass(base, parts)
        if step == 0:
            both = row_exchange(jnp.concatenate([row, tot]), npr)
            row, tot = both[:2], both[2:]
        else:
            row = row_exchange(row, npr)
        col = col_pass(base, row)
        col, have = lax.optimization_barrier((col, have))
        parts = col_exchange(col, nb)
        have, parts = lax.optimization_barrier((have, parts))
    for pair in plan:
        send_pair(have, pair, nb)
    row, code = row_last(kept, centers, parts)
    row = row_exchange(row, npr)
    row, have, centers = lax.optimization_barrier((row, have, centers))
    rows_all = gather_rows(jnp.concatenate([row, tot]), nb)
    embeds = pack([have[h][k] for k in range(0, nb, 2) for h in range(2)])
    col = (1.0 / sum(parts)).reshape(2, protos)
    half = share // 2
    quarter = half // 2

    def grads(at):
        c = lax.dynamic_slice_in_dim(col, at, half, axis=1)
        return grad_pass(cut(centers, at, half), embeds, rows_all, c)

    gf = [
        soft[v] * (GRAD / tot[v])[:, None] - code[1 - v] * (GRAD / row[1 - v])[:, None]
        for v in range(2)
    ]
    pair = halve_over_proto(gf[0], npr, 1)
    theirs = grads(chip * share + (1 - core) * half)
    theirs, pair, late, features, prototypes = lax.optimization_barrier(
        (theirs, pair, gf[1], features, prototypes)
    )
    theirs = swap(theirs, "batch", nb, 1)
    pair = halve_over_proto(pair[0] + pair[1], npr, 2)
    pair_late = halve_over_proto(late, npr, 1)
    mine = grads(chip * share + core * half)
    mine, theirs, pair, pair_late = lax.optimization_barrier((mine, theirs, pair, pair_late))
    grad = norm_back(mine + theirs, cut(prototypes, chip * share + core * half, half))

    have, plan = [{0: grad[:quarter]}, {0: grad[quarter:]}], gather_plan(nb)
    last = bits_of(npr)[-1]
    send_pair(have, plan.pop(0), nb)
    shard = shard_back(pair, features[0], npr)
    near = swap(shard, "proto", npr, last)
    late = halve_over_proto(pair_late[0] + pair_late[1], npr, 2)
    have, near, late = lax.optimization_barrier((have, near, late))
    send_pair(have, plan.pop(0), nb)
    shards = [spread_out([shard, near], npr), shard_back(late, features[1], npr)]
    near = swap(shards[1], "proto", npr, last)
    have, near, first_view = lax.optimization_barrier((have, near, shards[0]))
    twin = {(h, 0): swap(have[h][0], "batch", nb, 1) for h in range(2)}
    for p in plan:
        send_pair(have, p, nb)
    shards = [first_view, spread_out([shards[1], near], npr)]
    have, twin, shards = lax.optimization_barrier((have, twin, shards))
    out, where = [], []
    for k in have[0]:
        for h in range(2):
            at = (chip ^ (k // 2)) * share + h * quarter
            other = twin[h, k] if (h, k) in twin else swap(have[h][k], "batch", nb, 1)
            out += [have[h][k], other]
            where += [at + core * half, at + (1 - core) * half]
    grad_prototypes = place(out, where, protos)

    idx = lax.axis_index("proto")
    out, where = [], []
    for v in range(2):
        for k, x in shards[v].items():
            out.append(x)
            where.append(home(idx ^ k, npr, rows) + v * rows)
    return place(out, where, 2 * rows).reshape(2, rows, width), grad_prototypes


def solution(mesh):
    nb, npr = mesh.shape["batch"], mesh.shape["proto"]
    return jax.shard_map(
        lambda f, p: per_device(nb, npr, f, p),
        mesh=mesh,
        in_specs=(P(None, "batch", None), P("proto", None)),
        out_specs=(P(None, "batch", None), P("proto", None)),
        check_vma=False,
    )
```

```python
import jax
import jax.numpy as jnp
from jax import lax
from jax.experimental import pallas as pl
from jax.experimental.pallas import tpu as pltpu
from jax.sharding import PartitionSpec as P

ITERS = 3
LOG2E = 1.4426950408889634
SOFT = 10.0 * LOG2E
GRAD = 5.0
F32 = jnp.float32
BF16 = jnp.bfloat16
NT = (((1,), (1,)), ((), ()))


def tile_of(n, most):
    t = most
    while n % t:
        t //= 2
    return t


def params(mib):
    return pltpu.CompilerParams(vmem_limit_bytes=mib * 2**20)


def cost(flops, nbytes):
    return pl.CostEstimate(flops=flops, bytes_accessed=nbytes, transcendentals=0)


def lane_fold(x):
    total = x[:, :128]
    for j in range(1, x.shape[1] // 128):
        total = total + x[:, 128 * j : 128 * (j + 1)]
    return total


def sub_fold(x):
    total = x[:8]
    for j in range(1, x.shape[0] // 8):
        total = total + x[8 * j : 8 * (j + 1)]
    return total


def spread(row):
    return jnp.broadcast_to(row, (128, row.shape[1])).T


def unit_of(x):
    inv = lax.rsqrt(jnp.sum(x * x, axis=-1, keepdims=True) + 1e-06)
    return x * inv, inv


def two_terms(x):
    high = x.astype(BF16)
    return high, (x - high.astype(F32)).astype(BF16)


def in_hbm(x):
    return pltpu.with_memory_space_constraint(x, pltpu.HBM)


def in_vmem():
    return pl.BlockSpec(memory_space=pltpu.VMEM)


def first_kernel(feat_ref, proto_ref, lo_ref, hi_ref, cent_ref, col_ref, tot_ref, soft_ref, *refs):
    kept_ref, *base_refs, acc, embed_ref, sems = refs
    i = pl.program_id(0)
    rows = feat_ref.shape[1]
    kt = proto_ref.shape[0]
    rc = base_refs[0].shape[1]

    @pl.when(i == 0)
    def _():
        acc[...] = jnp.zeros_like(acc)
        soft_ref[...] = jnp.zeros_like(soft_ref)
        for v in range(2):
            e = unit_of(feat_ref[v].astype(F32))[0].astype(BF16)
            embed_ref[v] = e
            lo_ref[v] = e[: rows // 2].astype(F32)
            hi_ref[v] = e[rows // 2 :].astype(F32)

    cent_ref[...] = unit_of(proto_ref[...].astype(F32))[0].astype(BF16)
    for v in range(2):
        col = jnp.zeros((8, kt), F32)
        for j in range(rows // rc):
            r = slice(j * rc, (j + 1) * rc)
            s = lax.dot_general(embed_ref[v, r, :], cent_ref[...], NT, preferred_element_type=F32)
            e = jnp.exp2(s * SOFT)
            acc[v, r, :] += lane_fold(e)
            soft_ref[v, r, :] += jnp.dot(e.astype(BF16), cent_ref[...], preferred_element_type=F32)
            b = e * e
            base_refs[v * (rows // rc) + j][i] = b.astype(BF16)
            col = col + sub_fold(b)
        col_ref[v, pl.ds(i, 1), :] = jnp.sum(col, axis=0, keepdims=True)

    def keep(tile, j):
        return pltpu.make_async_copy(base_refs[j].at[tile], kept_ref.at[j, tile], sems.at[tile, j])

    for j in range(len(base_refs)):
        keep(i, j).start()

    @pl.when(i == pl.num_programs(0) - 1)
    def _():
        for tile in range(sems.shape[0]):
            for j in range(len(base_refs)):
                keep(tile, j).wait()
        for v in range(2):
            tot_ref[v : v + 1, :] = jnp.sum(acc[v].T, axis=0, keepdims=True)


def first(features, prototypes):
    _, rows, width = features.shape
    protos = prototypes.shape[0]
    kt = tile_of(protos, 1024)
    n = protos // kt
    rc = tile_of(rows, 256)
    m = 2 * rows // rc
    outs = pl.pallas_call(
        first_kernel,
        grid=(n,),
        in_specs=[in_vmem(), pl.BlockSpec((kt, width), lambda i: (i, 0))],
        out_specs=[
            in_vmem(),
            in_vmem(),
            pl.BlockSpec((kt, width), lambda i: (i, 0)),
            in_vmem(),
            in_vmem(),
            in_vmem(),
            pl.BlockSpec(memory_space=pl.ANY),
        ]
        + [in_vmem()] * m,
        out_shape=[
            jax.ShapeDtypeStruct((2, rows // 2, width), F32),
            jax.ShapeDtypeStruct((2, rows // 2, width), F32),
            jax.ShapeDtypeStruct((protos, width), BF16),
            jax.ShapeDtypeStruct((2, n, kt), F32),
            jax.ShapeDtypeStruct((2, rows), F32),
            jax.ShapeDtypeStruct((2, rows, width), F32),
            pltpu.HBM((m, n, rc, kt), BF16),
        ]
        + [pltpu.VMEM((n, rc, kt), BF16)] * m,
        scratch_shapes=[
            pltpu.VMEM((2, rows, 128), F32),
            pltpu.VMEM((2, rows, width), BF16),
            pltpu.SemaphoreType.DMA((n, m)),
        ],
        compiler_params=params(16),
        cost_estimate=cost(16 * rows * protos * width, 0),
        name="first",
    )(features, prototypes)
    return outs[:7], outs[7:]


def load_scales(part_refs, rows_ref, cols_ref, v):
    n, kt = rows_ref.shape
    half = kt // 2
    for i in range(n):
        c = 1.0 / sum(p[v, i : i + 1, :] for p in part_refs)
        rows_ref[i : i + 1, :] = c
        high, low = two_terms(c[:, half:])
        cols_ref[i] = jnp.concatenate([high, low, jnp.zeros((126, half), BF16)], axis=0).T


def block_sum(base_ref, rows_ref, cols_ref, acc):
    n, rc, kt = base_ref.shape
    half = kt // 2
    total = jnp.dot(base_ref[0, :, half:], cols_ref[0], preferred_element_type=F32)
    for i in range(1, n):
        total = total + jnp.dot(base_ref[i, :, half:], cols_ref[i], preferred_element_type=F32)
    acc[...] = total
    step = 32
    for j in range(0, rc, step):
        r = slice(j, j + step)
        part = acc[r]
        for i in range(n):
            part = part + lane_fold(base_ref[i, r, :half].astype(F32) * rows_ref[i : i + 1, :half])
        acc[r] = part
    return jnp.sum(acc[...].T, axis=0, keepdims=True)


def row_kernel(m, *refs):
    base_refs, part_refs = refs[:m], refs[m:-4]
    out_ref, rows_ref, cols_ref, acc = refs[-4:]
    rc = base_refs[0].shape[1]
    for v in range(2):
        load_scales(part_refs, rows_ref, cols_ref, v)
        for j in range(m // 2):
            sums = block_sum(base_refs[v * (m // 2) + j], rows_ref, cols_ref, acc)
            out_ref[v : v + 1, j * rc : (j + 1) * rc] = sums


def row_pass(base, parts):
    m = len(base)
    n, rc, kt = base[0].shape
    rows = m // 2 * rc
    return pl.pallas_call(
        lambda *refs: row_kernel(m, *refs),
        in_specs=[in_vmem()] * (m + len(parts)),
        out_specs=in_vmem(),
        out_shape=jax.ShapeDtypeStruct((2, rows), F32),
        scratch_shapes=[
            pltpu.VMEM((n, kt), F32),
            pltpu.VMEM((n, kt // 2, 128), BF16),
            pltpu.VMEM((rc, 128), F32),
        ],
        compiler_params=params(16),
        cost_estimate=cost(0, 4 * n * rows * kt),
        name="row_pass",
    )(*base, *parts)


def row_last_kernel(base_ref, cent_ref, *refs):
    *part_refs, out_ref, code_ref, acc = refs
    m, _, rc, _ = base_ref.shape
    i = pl.program_id(0)

    @pl.when(i == 0)
    def _():
        acc[...] = jnp.zeros_like(acc)
        code_ref[...] = jnp.zeros_like(code_ref)

    for v in range(2):
        c = 1.0 / sum(p[v, pl.ds(i, 1), :] for p in part_refs)
        for j in range(m // 2):
            r = slice(j * rc, (j + 1) * rc)
            w = base_ref[v * (m // 2) + j, 0].astype(F32) * c
            acc[v, r, :] += lane_fold(w)
            code_ref[v, r, :] += jnp.dot(w.astype(BF16), cent_ref[...], preferred_element_type=F32)

    @pl.when(i == pl.num_programs(0) - 1)
    def _():
        for v in range(2):
            out_ref[v : v + 1, :] = jnp.sum(acc[v].T, axis=0, keepdims=True)


def row_last(kept, centers, parts):
    m, n, rc, kt = kept.shape
    rows = m // 2 * rc
    width = centers.shape[1]
    return pl.pallas_call(
        row_last_kernel,
        grid=(n,),
        in_specs=[
            pl.BlockSpec((m, 1, rc, kt), lambda i: (0, i, 0, 0)),
            pl.BlockSpec((kt, width), lambda i: (i, 0)),
        ]
        + [in_vmem()] * len(parts),
        out_specs=[in_vmem()] * 2,
        out_shape=[
            jax.ShapeDtypeStruct((2, rows), F32),
            jax.ShapeDtypeStruct((2, rows, width), F32),
        ],
        scratch_shapes=[pltpu.VMEM((2, rows, 128), F32)],
        compiler_params=params(16),
        cost_estimate=cost(0, 8 * n * rows * kt),
        name="row_last",
    )(in_hbm(kept), in_hbm(centers), *parts)


def col_kernel(total_ref, *refs):
    *base_refs, out_ref = refs
    m = len(base_refs) // 2
    n, rc, kt = base_refs[0].shape
    for v in range(2):
        high, low = two_terms(1.0 / total_ref[v : v + 1, :])
        r = jnp.concatenate([high, low, jnp.zeros((14, m * rc), BF16)], axis=0)
        for i in range(n):
            total = jnp.zeros((16, kt), F32)
            for j in range(m):
                total = total + jnp.dot(
                    r[:, j * rc : (j + 1) * rc],
                    base_refs[v * m + j][i],
                    preferred_element_type=F32,
                )
            out_ref[v, i : i + 1, :] = total[0:1] + total[1:2]


def col_pass(base, total):
    n, rc, kt = base[0].shape
    m = len(base)
    return pl.pallas_call(
        col_kernel,
        in_specs=[in_vmem()] * (m + 1),
        out_specs=in_vmem(),
        out_shape=jax.ShapeDtypeStruct((2, n, kt), F32),
        compiler_params=params(16),
        cost_estimate=cost(0, 4 * n * m // 2 * rc * kt),
        name="col_pass",
    )(total, *base)


def pack_kernel(*refs):
    *part_refs, out_ref = refs
    for j, p in enumerate(part_refs):
        out_ref[j] = p[...].astype(BF16)


def pack(parts):
    _, rc, width = parts[0].shape
    m = len(parts)
    return pl.pallas_call(
        pack_kernel,
        grid=(2,),
        in_specs=[pl.BlockSpec((1, rc, width), lambda v: (v, 0, 0))] * m,
        out_specs=pl.BlockSpec((m, 1, rc, width), lambda v: (0, v, 0, 0)),
        out_shape=jax.ShapeDtypeStruct((m, 2, rc, width), BF16),
        compiler_params=params(32),
        cost_estimate=cost(0, 12 * m * rc * width),
        name="pack",
    )(*parts)


def grad_kernel(cent_ref, col_ref, embed, *refs):
    *row_refs, out_ref, scale = refs
    m, _, rc, _ = embed.shape
    i = pl.program_id(0)
    for v in range(2):
        scale[v] = spread(col_ref[v, pl.ds(i, 1), :])
    total = jnp.zeros(out_ref.shape, F32)
    for j in range(m):
        es = []
        for v in range(2):
            s = lax.dot_general(cent_ref[...], embed[j, v], NT, preferred_element_type=F32)
            es.append(jnp.exp2(s * SOFT))
        for v in range(2):
            o = 1 - v
            c = jnp.concatenate([scale[o]] * (rc // 128), axis=1)
            r = slice(j % 2 * rc, (j % 2 + 1) * rc)
            codes = es[o] * es[o] * (GRAD / row_refs[j // 2][o : o + 1, r]) * c
            g = (es[v] * (GRAD / row_refs[j // 2][2 + v : 3 + v, r]) - codes).astype(BF16)
            total = total + jnp.dot(g, embed[j, v], preferred_element_type=F32)
    out_ref[...] = total


def grad_pass(centers, embeds, row, col):
    protos, width = centers.shape
    m, _, rc, _ = embeds.shape
    kt = tile_of(protos, 512)
    n = protos // kt
    whole = lambda *s: pl.BlockSpec(s, lambda i: (0,) * len(s))
    return pl.pallas_call(
        grad_kernel,
        grid=(n,),
        in_specs=[
            pl.BlockSpec((kt, width), lambda i: (i, 0)),
            whole(2, n, kt),
            whole(m, 2, rc, width),
        ]
        + [whole(4, 2 * rc)] * (m // 2),
        out_specs=pl.BlockSpec((kt, width), lambda i: (i, 0)),
        out_shape=jax.ShapeDtypeStruct((protos, width), F32),
        scratch_shapes=[pltpu.VMEM((2, kt, 128), F32)],
        compiler_params=params(48),
        cost_estimate=cost(8 * protos * m * rc * width, 4 * m * rc * width),
        name="grad_pass",
    )(centers, col.reshape(2, n, kt), embeds, *row)


def place_kernel(at_ref, *refs):
    m = len(refs) - 2
    out_ref, sems = refs[m], refs[m + 1]
    copies = []
    for j in range(m):
        size = refs[j].shape[0]
        where = pl.ds(pl.multiple_of(at_ref[j], 8), size)
        copies.append(pltpu.make_async_copy(refs[j], out_ref.at[where], sems.at[j]))
    for c in copies:
        c.start()
    for c in copies:
        c.wait()


def place(pieces, at, size):
    m = len(pieces)
    return pl.pallas_call(
        place_kernel,
        in_specs=[pl.BlockSpec(memory_space=pltpu.SMEM)]
        + [pl.BlockSpec(memory_space=pltpu.VMEM)] * m,
        out_specs=pl.BlockSpec(memory_space=pl.ANY),
        out_shape=jax.ShapeDtypeStruct((size, pieces[0].shape[1]), F32),
        scratch_shapes=[pltpu.SemaphoreType.DMA((m,))],
        compiler_params=params(24),
        cost_estimate=cost(0, 12 * size * pieces[0].shape[1]),
        name="place",
    )(jnp.stack(at).astype(jnp.int32), *pieces)


def swap(x, axis, n, m):
    return lax.ppermute(x, axis, [(i, i ^ m) for i in range(n)])


def col_exchange(x, n):
    if n > 1:
        x = x + swap(x, "batch", n, 1)
    m = 2
    while n // m > 4:
        x = x + swap(x, "batch", n, m)
        m *= 2
    return [x] + [swap(x, "batch", n, k * m) for k in range(1, n // m)]


def row_exchange(x, n):
    m = 1
    while m < n:
        x = x + swap(x, "proto", n, m)
        m *= 2
    return x


def gather_plan(n):
    bits = [2**j for j in range(1, n.bit_length()) if 2**j < n]
    plan, keys_a, keys_b = [], [0], [0]
    for m, w in zip(bits, bits[::-1]):
        plan += [((k, m), (q, w)) for k, q in zip(keys_a, keys_b)]
        keys_a, keys_b = keys_a + [k ^ m for k in keys_a], keys_b + [k ^ w for k in keys_b]
    return plan


def send_pair(have, pair, n):
    for h, (k, m) in zip(have, pair):
        h[k ^ m] = swap(h[k], "batch", n, m)


def gather_rows(x, n):
    return [x] + [swap(x, "batch", n, k) for k in range(2, n, 2)]


def norm_back(grad, given):
    x = given.astype(F32)
    inverse = lax.rsqrt(jnp.sum(x * x, axis=-1, keepdims=True) + 1e-06)
    unit = x * inverse
    return inverse * (grad - unit * jnp.sum(unit * grad, axis=-1, keepdims=True))


def cut(x, at, size):
    return lax.dynamic_slice_in_dim(x, at, size, axis=0)


def halve_over_proto(x, n, m=1):
    keep, give = halves_over_proto(x, m)
    return keep, swap(give, "proto", n, m)


def halves_over_proto(x, m):
    size = x.shape[0] // 2
    side = (lax.axis_index("proto") // m) % 2
    return cut(x, side * size, size), cut(x, (1 - side) * size, size)


def home(i, n, size):
    at = 0 * i
    for m in bits_of(n):
        size //= 2
        at = at + (i // m) % 2 * size
    return at


def spread_out(pieces, n):
    bits = bits_of(n)[::-1]
    keys = [0, bits[0]]
    size = pieces[0].shape[0]
    x = jnp.concatenate(pieces, axis=0)
    for m in bits[1:-1]:
        x = jnp.concatenate([x, swap(x, "proto", n, m)], axis=0)
        keys = keys + [k ^ m for k in keys]
    y = swap(x, "proto", n, bits[-1])
    found = {}
    for j, k in enumerate(keys):
        found[k] = x[j * size : (j + 1) * size]
        found[k ^ bits[-1]] = y[j * size : (j + 1) * size]
    return found


def bits_of(n):
    return [2**j for j in range(n.bit_length()) if 2**j < n]


def shard_back(pair, given, n):
    x = pair[0] + pair[1]
    for m in bits_of(n)[2:]:
        a, b = halve_over_proto(x, n, m)
        x = a + b
    at = home(lax.axis_index("proto"), n, given.shape[0])
    return norm_back(x, cut(given, at, x.shape[0]))


def per_device(nb, npr, features, prototypes):
    _, rows, width = features.shape
    protos = prototypes.shape[0]
    me = lax.axis_index("batch")
    chip, core = me // 2, me % 2
    share = protos // (nb // 2)

    (lo, hi, centers, col, tot, soft, kept), base = first(features, prototypes)
    parts = col_exchange(col, nb)
    have, plan = [{0: lo}, {0: hi}], gather_plan(nb)
    have, parts = lax.optimization_barrier((have, parts))
    for step in range(ITERS - 1):
        if plan:
            send_pair(have, plan.pop(0), nb)
        row = row_pass(base, parts)
        if step == 0:
            both = row_exchange(jnp.concatenate([row, tot]), npr)
            row, tot = both[:2], both[2:]
        else:
            row = row_exchange(row, npr)
        col = col_pass(base, row)
        col, have = lax.optimization_barrier((col, have))
        parts = col_exchange(col, nb)
        have, parts = lax.optimization_barrier((have, parts))
    for pair in plan:
        send_pair(have, pair, nb)
    row, code = row_last(kept, centers, parts)
    row = row_exchange(row, npr)
    row, have, centers = lax.optimization_barrier((row, have, centers))
    rows_all = gather_rows(jnp.concatenate([row, tot]), nb)
    embeds = pack([have[h][k] for k in range(0, nb, 2) for h in range(2)])
    col = (1.0 / sum(parts)).reshape(2, protos)
    half = share // 2
    quarter = half // 2

    def grads(at):
        c = lax.dynamic_slice_in_dim(col, at, half, axis=1)
        return grad_pass(cut(centers, at, half), embeds, rows_all, c)

    gf = [
        soft[v] * (GRAD / tot[v])[:, None] - code[1 - v] * (GRAD / row[1 - v])[:, None]
        for v in range(2)
    ]
    pair = halve_over_proto(gf[0], npr, 1)
    theirs = grads(chip * share + (1 - core) * half)
    theirs, pair, late, features, prototypes = lax.optimization_barrier(
        (theirs, pair, gf[1], features, prototypes)
    )
    theirs = swap(theirs, "batch", nb, 1)
    keep, give = halves_over_proto(pair[0] + pair[1], 2)
    keep_late, give_late = halves_over_proto(late, 1)
    give, give_late, embeds = lax.optimization_barrier((give, give_late, embeds))
    pair = keep, swap(give, "proto", npr, 2)
    pair_late = keep_late, swap(give_late, "proto", npr, 1)
    mine = grads(chip * share + core * half)
    mine, theirs, pair, pair_late = lax.optimization_barrier((mine, theirs, pair, pair_late))
    grad = norm_back(mine + theirs, cut(prototypes, chip * share + core * half, half))

    have, plan = [{0: grad[:quarter]}, {0: grad[quarter:]}], gather_plan(nb)
    last = bits_of(npr)[-1]
    send_pair(have, plan.pop(0), nb)
    shard = shard_back(pair, features[0], npr)
    near = swap(shard, "proto", npr, last)
    late = halve_over_proto(pair_late[0] + pair_late[1], npr, 2)
    have, near, late = lax.optimization_barrier((have, near, late))
    send_pair(have, plan.pop(0), nb)
    shards = [spread_out([shard, near], npr), shard_back(late, features[1], npr)]
    near = swap(shards[1], "proto", npr, last)
    have, near, first_view = lax.optimization_barrier((have, near, shards[0]))
    twin = {(h, 0): swap(have[h][0], "batch", nb, 1) for h in range(2)}
    for p in plan:
        send_pair(have, p, nb)
    shards = [first_view, spread_out([shards[1], near], npr)]
    have, twin, shards = lax.optimization_barrier((have, twin, shards))
    out, where = [], []
    for k in have[0]:
        for h in range(2):
            at = (chip ^ (k // 2)) * share + h * quarter
            other = twin[h, k] if (h, k) in twin else swap(have[h][k], "batch", nb, 1)
            out += [have[h][k], other]
            where += [at + core * half, at + (1 - core) * half]
    grad_prototypes = place(out, where, protos)

    idx = lax.axis_index("proto")
    out, where = [], []
    for v in range(2):
        for k, x in shards[v].items():
            out.append(x)
            where.append(home(idx ^ k, npr, rows) + v * rows)
    return place(out, where, 2 * rows).reshape(2, rows, width), grad_prototypes


def solution(mesh):
    nb, npr = mesh.shape["batch"], mesh.shape["proto"]
    return jax.shard_map(
        lambda f, p: per_device(nb, npr, f, p),
        mesh=mesh,
        in_specs=(P(None, "batch", None), P("proto", None)),
        out_specs=(P(None, "batch", None), P("proto", None)),
        check_vma=False,
    )
```
